32 devices in a mesh: row: 4 (over y, x), col: 8 (over z, core).
Axes of the slice: x: 2, y: 2, z: 4, core: 2. Of those that a mesh axis runs over, the one named last changes fastest.
Arguments:
- rhs: float32 [4, 4, 512, 2, 8, 512], P(None, 'row', None, None, 'col'), may hold values from -6 to 6, as said below
- panels: bfloat16 [2, 4, 4, 512, 1024], P(None, None, 'row', 'col'), may hold values from -6 to 6, as said below
- inverses: float32 [3, 512, 512], replicated, may hold values from -2 to 2, as said below
Outputs:
- new_rhs: float32 [4, 4, 512, 2, 8, 512], P(None, 'row', None, None, 'col')
- solved: float32 [2, 512, 512], P(None, 'row', 'col')
The draws below stay inside these ranges and needn't reach their ends.
Inputs may be any that keep to these rules, and one draw needn't show every extreme that they name: rhs is symmetric as a matrix of order 16 * 512. `panels`: A and E are upper triangular: panel rows of block n are zero in the first 512 columns, and the diagonal blocks (m,m) and (n,n) are upper triangular with positive diagonals. The inverses are upper triangular preconditioners, only near the true inverses, and are used as given.
All inputs are finite; a program needn't handle non-finite values.
Results may differ from the reference program's by a relative error of at most 0.0025.
Values may be sent and summed in bfloat16 or wider, within the bound.
A program may use at most 128 MiB of HBM per device.

```python
import math
import jax
import jax.numpy as jnp
from jax import lax

B = 512
BCOL = 2
SWEEPS = 3
BLOCKS = 16
RB = 4


def diag_parts(key):
    seeds = jax.random.split(jax.random.fold_in(key, 7), 4)
    scale_a = jnp.exp(jax.random.uniform(seeds[0], (2, B), jnp.float32, 0.0, math.log(2.0)))
    ratio = jnp.exp(jax.random.uniform(seeds[1], (2, B), jnp.float32, math.log(0.8), math.log(1.25)))
    scale_e = scale_a * ratio
    strict = jnp.triu(jnp.ones((B, B), jnp.float32), 1)
    ident = jnp.eye(B, dtype=jnp.float32)
    upper_a = jax.random.normal(seeds[2], (2, B, B), jnp.float32) * (0.3 / math.sqrt(B)) * strict
    upper_e = jax.random.normal(seeds[3], (2, B, B), jnp.float32) * (0.3 / math.sqrt(B)) * strict
    blocks_a = scale_a[:, :, None] * (ident + upper_a)
    blocks_e = scale_e[:, :, None] * (ident + upper_e)
    noise_seeds = jax.random.split(jax.random.fold_in(key, 13), 4)
    diag_noise_a = jax.random.uniform(noise_seeds[0], (2, B), jnp.float32, -0.08, 0.08)
    diag_noise_e = jax.random.uniform(noise_seeds[1], (2, B), jnp.float32, -0.08, 0.08)
    extra_a = jnp.clip(jax.random.normal(noise_seeds[2], (2, B, B), jnp.float32), -6.0, 6.0) * (0.1 / math.sqrt(B)) * strict
    extra_e = jnp.clip(jax.random.normal(noise_seeds[3], (2, B, B), jnp.float32), -6.0, 6.0) * (0.1 / math.sqrt(B)) * strict
    approx_a = (ident * (1.0 + diag_noise_a[:, None, :]) - upper_a + extra_a) / scale_a[:, None, :]
    approximate_second_matrix = (ident * (1.0 + diag_noise_e[:, None, :]) - upper_e + extra_e) / scale_e[:, None, :]
    return (blocks_a, blocks_e, approx_a, approximate_second_matrix)


def draw_rhs(key, part):
    matrix_order = BLOCKS * B
    raw_values = jax.random.normal(key, (matrix_order, matrix_order), jnp.float32)
    symmetric = jnp.clip((raw_values + raw_values.T) * 0.7071, -6.0, 6.0)
    return symmetric.reshape(RB, BLOCKS // RB, B, BCOL, BLOCKS // BCOL, B)


def draw_panels(key, part):
    blocks_a, blocks_e, approx_a, approximate_second_matrix = diag_parts(key)
    dense_key = jax.random.fold_in(key, 11)
    matrix_order = BLOCKS * B
    dense = jnp.clip(jax.random.normal(dense_key, (2, matrix_order, 2 * B), jnp.float32), -6.0, 6.0)
    dense = dense * (1.0 / math.sqrt(B))
    last_start = matrix_order - B
    prev_start = last_start - B
    dense = dense.at[0, prev_start:last_start, :B].set(blocks_a[0])
    dense = dense.at[1, prev_start:last_start, :B].set(blocks_e[0])
    dense = dense.at[:, last_start:, :B].set(0.0)
    dense = dense.at[0, last_start:, B:].set(blocks_a[1])
    dense = dense.at[1, last_start:, B:].set(blocks_e[1])
    return dense.reshape(2, RB, BLOCKS // RB, B, 2 * B).astype(jnp.bfloat16)


def draw_inverses(key, part):
    blocks_a, blocks_e, approx_a, approximate_second_matrix = diag_parts(key)
    return jnp.stack([approx_a[0], approx_a[1], approximate_second_matrix[1]])


def setup_inputs(seed: int = 0) -> dict:
    splits = jax.random.split(jax.random.key(seed), 4)
    rhs = draw_rhs(jax.random.fold_in(splits[3], 71), 0)
    panels = draw_panels(jax.random.fold_in(splits[3], 71), 0)
    inverses = draw_inverses(jax.random.fold_in(splits[3], 71), 0)
    return {"rhs": rhs, "panels": panels, "inverses": inverses}


def product(left, right):
    return jnp.dot(left, right, precision=lax.Precision.HIGHEST, preferred_element_type=jnp.float32)


def reference(rhs, panels, inverses):
    matrix_order = BLOCKS * B
    matrix_rhs = rhs.reshape(matrix_order, matrix_order)
    panel_a = panels[0].reshape(matrix_order, 2 * B)
    panel_e = panels[1].reshape(matrix_order, 2 * B)
    last_start = matrix_order - B
    prev_start = last_start - B
    a_last = panel_a[last_start:, B:].astype(jnp.float32)
    e_last = panel_e[last_start:, B:].astype(jnp.float32)
    a_upper = panel_a[prev_start:last_start, B:].astype(jnp.float32)
    e_upper = panel_e[prev_start:last_start, B:].astype(jnp.float32)
    a_diag = panel_a[prev_start:last_start, :B].astype(jnp.float32)
    e_diag = panel_e[prev_start:last_start, :B].astype(jnp.float32)
    rhs_last = matrix_rhs[last_start:, last_start:]
    rhs_upper = matrix_rhs[prev_start:last_start, last_start:]
    diag_solution = jnp.zeros((B, B), jnp.float32)
    for sweep_index in range(SWEEPS):
        left_term = product(product(a_last, diag_solution), e_last.T)
        residual = -rhs_last - (left_term + left_term.T)
        update_term = product(product(inverses[1], residual), inverses[2].T)
        diag_solution = diag_solution + 0.25 * (update_term + update_term.T)
    target = -rhs_upper - (product(product(a_upper, diag_solution), e_last.T) + product(product(e_upper, diag_solution), a_last.T))
    next_solution = jnp.zeros((B, B), jnp.float32)
    for sweep_index in range(SWEEPS):
        residual = target - (product(product(a_diag, next_solution), e_last.T) + product(product(e_diag, next_solution), a_last.T))
        next_solution = next_solution + 0.5 * product(product(inverses[0], residual), inverses[2].T)
    solved = jnp.stack([diag_solution, next_solution])
    zero_block = jnp.zeros((B, B), jnp.float32)
    known_block = jnp.concatenate([jnp.concatenate([zero_block, next_solution], 1), jnp.concatenate([next_solution.T, diag_solution], 1)], 0).astype(jnp.bfloat16)
    z_panel = jnp.dot(panel_a, known_block, preferred_element_type=jnp.float32).astype(jnp.bfloat16)
    first_term = jnp.dot(z_panel, panel_e.T, preferred_element_type=jnp.float32)
    second_term = jnp.dot(panel_e, z_panel.T, preferred_element_type=jnp.float32)
    new_rhs = (matrix_rhs + first_term + second_term).reshape(rhs.shape)
    return new_rhs, solved
```

```python
import functools

import jax
import jax.numpy as jnp
from jax import lax
from jax.experimental import pallas as pl
from jax.experimental.pallas import tpu as pltpu
from jax.sharding import PartitionSpec as P

SWEEPS = 3
LANES = 128
MESH = pl.DeviceIdType.MESH
VMEM_LIMIT = 50 * 1024 * 1024


def remote(src, dst, send_sem, recv_sem, row, col):
    return pltpu.make_async_remote_copy(
        src_ref=src, dst_ref=dst, send_sem=send_sem, recv_sem=recv_sem,
        device_id=(row, col), device_id_type=MESH,
    )


def greet(partners):
    barrier = pltpu.get_barrier_semaphore()
    for row, col in partners:
        pl.semaphore_signal(barrier, inc=1, device_id=(row, col), device_id_type=MESH)
    pl.semaphore_wait(barrier, len(partners))


def corner_kernel(
    row_count, col_count, last_ref, g_ref, upper, lower, g_out,
    send_upper, send_lower, send_sibling, send_g1, send_g2, send_g3, send_g4,
    recv_corner, recv_sibling, recv_g1, recv_g2, recv_g3, recv_g4, local_sem,
):
    row = lax.axis_index("row")
    col = lax.axis_index("col")
    core = lax.rem(col, 2)
    sibling = col + 1 - 2 * core
    size = g_ref.shape[0]
    half = size // 2
    part = size // row_count
    last_col = col_count - 1
    other_rows = [lax.rem(row + j, row_count) for j in range(1, row_count)]
    other_cols = [lax.rem(col + 2 * j, col_count) for j in range(1, col_count // 2)]
    greet([(r, col) for r in other_rows] + [(row, c) for c in other_cols] + [(row, sibling)])

    here = pl.ds(pl.multiple_of(core * half, half), half)
    there = pl.ds(pl.multiple_of((1 - core) * half, half), half)

    def rows_of(index):
        return pl.ds(pl.multiple_of(index * part, part), part)

    corners = (
        (row_count - 2, last_ref.at[:, here, :], upper, send_upper, 0),
        (row_count - 1, last_ref.at[:, here, pl.ds(size, size)], lower, send_lower, 1),
    )
    for source_row, src, out, send, slot in corners:
        dst = out.at[:, here, :]

        @pl.when(row == source_row)
        def _():
            pltpu.make_async_copy(src, dst, local_sem.at[slot]).start()
            for j, r in enumerate(other_rows):
                remote(src, dst, send.at[j], recv_corner.at[slot], r, col).start()

        @pl.when(jnp.logical_and(row == source_row, col == last_col))
        def _():
            mine = rows_of(row)
            pltpu.make_async_copy(
                g_ref.at[mine, :], g_out.at[slot, mine, :], local_sem.at[2 + slot]
            ).start()
            for j, r in enumerate(other_rows):
                theirs = rows_of(r)
                remote(
                    g_ref.at[theirs, :], g_out.at[slot, theirs, :],
                    send_g1.at[slot, j], recv_g1.at[slot], r, col,
                ).start()

    mine = rows_of(row)
    g_mine = g_out.at[:, mine, :]

    @pl.when(col == last_col)
    def _():
        for source_row, src, out, send, slot in corners:
            piece = g_out.at[slot, mine, :]

            @pl.when(row == source_row)
            def _():
                pltpu.make_async_copy(g_ref.at[mine, :], piece, local_sem.at[2 + slot]).wait()

            @pl.when(row != source_row)
            def _():
                remote(piece, piece, send_g1.at[slot, 0], recv_g1.at[slot], row, col).wait_recv()

        for j, c in enumerate(other_cols):
            remote(g_mine, g_mine, send_g2.at[j], recv_g2, row, c).start()

    for source_row, src, out, send, slot in corners:
        dst = out.at[:, here, :]

        @pl.when(row == source_row)
        def _():
            pltpu.make_async_copy(src, dst, local_sem.at[slot]).wait()

        @pl.when(row != source_row)
        def _():
            remote(dst, dst, send.at[0], recv_corner.at[slot], row, col).wait_recv()

        remote(dst, dst, send_sibling.at[slot], recv_sibling.at[slot], row, sibling).start()

    @pl.when(core == 1)
    def _():
        @pl.when(col != last_col)
        def _():
            remote(g_mine, g_mine, send_g2.at[0], recv_g2, row, col).wait_recv()

        for j, r in enumerate(other_rows):
            remote(g_mine, g_mine, send_g3.at[j], recv_g3.at[row], r, col).start()
        for r in other_rows:
            piece = g_out.at[:, rows_of(r), :]
            remote(piece, piece, send_g3.at[0], recv_g3.at[r], row, col).wait_recv()
        remote(g_out, g_out, send_g4, recv_g4, row, sibling).start()

    @pl.when(core == 0)
    def _():
        remote(g_out, g_out, send_g4, recv_g4, row, sibling).wait_recv()

    for source_row, src, out, send, slot in corners:
        dst = out.at[:, here, :]
        arriving = out.at[:, there, :]
        remote(arriving, arriving, send_sibling.at[slot], recv_sibling.at[slot], row, sibling).wait_recv()
        remote(dst, dst, send_sibling.at[slot], recv_sibling.at[slot], row, sibling).wait_send()

        @pl.when(row == source_row)
        def _():
            for j, r in enumerate(other_rows):
                remote(src, dst, send.at[j], recv_corner.at[slot], r, col).wait_send()

        @pl.when(jnp.logical_and(row == source_row, col == last_col))
        def _():
            for j, r in enumerate(other_rows):
                theirs = rows_of(r)
                remote(
                    g_ref.at[theirs, :], g_out.at[slot, theirs, :],
                    send_g1.at[slot, j], recv_g1.at[slot], r, col,
                ).wait_send()

    @pl.when(col == last_col)
    def _():
        for j, c in enumerate(other_cols):
            remote(g_mine, g_mine, send_g2.at[j], recv_g2, row, c).wait_send()

    @pl.when(core == 1)
    def _():
        for j, r in enumerate(other_rows):
            remote(g_mine, g_mine, send_g3.at[j], recv_g3.at[row], r, col).wait_send()
        remote(g_out, g_out, send_g4, recv_g4, row, sibling).wait_send()


def share_corner(last_rows, rhs_last, row_count, col_count):
    size = rhs_last.shape[0]
    dma = pltpu.SemaphoreType.DMA
    peers = row_count - 1
    return pl.pallas_call(
        functools.partial(corner_kernel, row_count, col_count),
        out_shape=(
            jax.ShapeDtypeStruct((2, size, 2 * size), jnp.bfloat16),
            jax.ShapeDtypeStruct((2, size, size), jnp.bfloat16),
            jax.ShapeDtypeStruct((2, size, size), jnp.float32),
        ),
        in_specs=[pl.BlockSpec(memory_space=pl.ANY)] * 2,
        out_specs=[pl.BlockSpec(memory_space=pl.ANY)] * 3,
        scratch_shapes=[
            dma((peers,)), dma((peers,)), dma((2,)), dma((2, peers)),
            dma((col_count // 2,)), dma((peers,)), dma,
            dma((2,)), dma((2,)), dma((2,)), dma, dma((row_count,)), dma, dma((4,)),
        ],
        compiler_params=pltpu.CompilerParams(collective_id=0, has_side_effects=True),
        cost_estimate=pl.CostEstimate(flops=0, bytes_accessed=60_000_000, transcendentals=0),
    )(last_rows, rhs_last)


def mm(left, right):
    return lax.dot_general(left, right, (((1,), (0,)), ((), ())), preferred_element_type=jnp.float32)


def mm_t(left, right):
    return lax.dot_general(left, right, (((1,), (1,)), ((), ())), preferred_element_type=jnp.float32)


def split(value):
    high = value.astype(jnp.bfloat16)
    low = (value - high.astype(jnp.float32)).astype(jnp.bfloat16)
    return high, low


def upper_times(tri, parts):
    half = tri[0].shape[0] // 2
    top = bottom = None
    for i, t in enumerate(tri):
        for j, p in enumerate(parts):
            if i + j < 2:
                a = mm(t[:half], p)
                b = mm(t[half:, half:], p[half:])
                top = a if top is None else top + a
                bottom = b if bottom is None else bottom + b
    return jnp.concatenate([top, bottom], 0)


def times_upper_t(parts, tri):
    half = tri[0].shape[0] // 2
    left = right = None
    for i, t in enumerate(tri):
        for j, p in enumerate(parts):
            if i + j < 2:
                a = mm_t(p, t[:half])
                b = mm_t(p[:, half:], t[half:, half:])
                left = a if left is None else left + a
                right = b if right is None else right + b
    return jnp.concatenate([left, right], 1)


def solve_kernel(upper, lower, g, inverses, out, inv_high, inv_low):
    size = g.shape[1]
    for i in range(3):
        high, low = split(inverses[i])
        inv_high[i] = high
        inv_low[i] = low

    def precondition(i, residual):
        first = upper_times((inv_high[i], inv_low[i]), split(residual))
        return times_upper_t(split(first), (inv_high[2], inv_low[2]))

    def corner_update(residual):
        update = precondition(1, residual)
        return 0.25 * (update + update.T)

    out[0] = corner_update(-g[1])

    def corner_sweep(_, carry):
        first = upper_times((lower[0],), split(out[0]))
        term = times_upper_t(split(first), (lower[1],))
        out[0] = out[0] + corner_update(-g[1] - (term + term.T))
        return carry

    lax.fori_loop(1, SWEEPS, corner_sweep, 0)

    parts = split(out[0])
    over_a = split(sum(mm(upper[0, :, size:], p) for p in parts))
    over_e = split(sum(mm(upper[1, :, size:], p) for p in parts))
    g[0] = -g[0] - (times_upper_t(over_a, (lower[1],)) + times_upper_t(over_e, (lower[0],)))
    out[1] = 0.5 * precondition(0, g[0])

    def upper_sweep(_, carry):
        held = split(out[1])
        by_a = split(upper_times((upper[0, :, :size],), held))
        by_e = split(upper_times((upper[1, :, :size],), held))
        term = times_upper_t(by_a, (lower[1],)) + times_upper_t(by_e, (lower[0],))
        out[1] = out[1] + 0.5 * precondition(0, g[0] - term)
        return carry

    lax.fori_loop(1, SWEEPS, upper_sweep, 0)


def solve(upper, lower, g, inverses):
    size = g.shape[1]
    return pl.pallas_call(
        solve_kernel,
        out_shape=jax.ShapeDtypeStruct((2, size, size), jnp.float32),
        in_specs=[pl.BlockSpec(memory_space=pltpu.VMEM)] * 4,
        out_specs=pl.BlockSpec(memory_space=pltpu.VMEM),
        scratch_shapes=[
            pltpu.VMEM((3, size, size), jnp.bfloat16),
            pltpu.VMEM((3, size, size), jnp.bfloat16),
        ],
        compiler_params=pltpu.CompilerParams(vmem_limit_bytes=VMEM_LIMIT),
        cost_estimate=pl.CostEstimate(
            flops=100 * size ** 3, bytes_accessed=100_000_000, transcendentals=0
        ),
    )(upper, lower, g, inverses)


def gray(index):
    return index ^ (index >> 1)


def column_kernel(row_count, chosen, out, send, recv, local_sem):
    row = lax.axis_index("row")
    col = lax.axis_index("col")
    source = lax.rem(col, row_count)
    matrices, blocks, size, _ = chosen.shape
    part = size // 4
    chunks = [
        (m, b, pl.ds(p * part, part)) for b in range(blocks) for p in range(4) for m in range(matrices)
    ]
    places = [gray(i) for i in range(row_count)]

    def at_place(place):
        value = jnp.int32(0)
        for s in range(row_count):
            value = jnp.where(source == s, s ^ places[place], value)
        return value

    chain = [at_place(i) for i in range(row_count)]
    barrier = pltpu.get_barrier_semaphore()
    for i in range(row_count):

        @pl.when(row == chain[i])
        def _():
            around = [chain[j] for j in (i - 1, i + 1) if 0 <= j < row_count]
            for r in around:
                pl.semaphore_signal(barrier, inc=1, device_id=(r, col), device_id_type=MESH)
            pl.semaphore_wait(barrier, len(around))
            if i == 0:
                pltpu.make_async_copy(chosen, out, local_sem).start()
            for n, (m, b, rows) in enumerate(chunks):
                dst = out.at[m, b, rows, :]
                src = chosen.at[m, b, rows, :] if i == 0 else dst
                if i > 0:
                    remote(dst, dst, send.at[n], recv.at[n], row, col).wait_recv()
                if i < row_count - 1:
                    remote(src, dst, send.at[n], recv.at[n], chain[i + 1], col).start()
            if i == 0:
                pltpu.make_async_copy(chosen, out, local_sem).wait()
            if i < row_count - 1:
                for n, (m, b, rows) in enumerate(chunks):
                    dst = out.at[m, b, rows, :]
                    src = chosen.at[m, b, rows, :] if i == 0 else dst
                    remote(src, dst, send.at[n], recv.at[n], chain[i + 1], col).wait_send()


def share_columns(chosen, row_count):
    count = chosen.shape[0] * chosen.shape[1] * 4
    dma = pltpu.SemaphoreType.DMA
    return pl.pallas_call(
        functools.partial(column_kernel, row_count),
        out_shape=jax.ShapeDtypeStruct(chosen.shape, chosen.dtype),
        in_specs=[pl.BlockSpec(memory_space=pl.ANY)],
        out_specs=pl.BlockSpec(memory_space=pl.ANY),
        scratch_shapes=[dma((count,)), dma((count,)), dma],
        compiler_params=pltpu.CompilerParams(collective_id=1, has_side_effects=True),
        cost_estimate=pl.CostEstimate(flops=0, bytes_accessed=60_000_000, transcendentals=0),
    )(chosen)


def update_kernel(
    rest_steps, rest_ref, last_ref, cols_ref, x_ref, rhs_ref, out_ref, x_high, x_turned, z_cols
):
    step = pl.program_id(0)
    size = x_ref.shape[1]
    tile = rest_ref.shape[1]
    groups = rhs_ref.shape[0] // tile

    def times_known(left):
        from_right = left[:, size:]
        first = mm(from_right, x_turned[...])
        second = mm(left[:, :size], x_high[1]) + mm(from_right, x_high[0])
        return jnp.concatenate([first, second], 1).astype(jnp.bfloat16)

    @pl.when(step == 0)
    def _():
        x_high[...] = x_ref[...].astype(jnp.bfloat16)
        x_turned[...] = x_ref[1].T.astype(jnp.bfloat16)
        for b in range(z_cols.shape[0]):
            z_cols[b] = times_known(cols_ref[0, b])

    def work(rows_ref):
        z_rows = times_known(rows_ref[0])
        for b in range(z_cols.shape[0]):
            total = mm_t(z_rows, cols_ref[1, b]) + mm_t(rows_ref[1], z_cols[b])
            for q in range(size // LANES):
                where = pl.ds(b * (size // LANES) + q, tile, stride=groups)
                out_ref[where, :] = rhs_ref[where, :] + total[:, q * LANES:(q + 1) * LANES]

    @pl.when(step < rest_steps)
    def _():
        work(rest_ref)

    @pl.when(step >= rest_steps)
    def _():
        work(last_ref)


def update(rest, last, cols, x, rhs):
    size = x.shape[1]
    width = rest.shape[-1]
    blocks = cols.shape[1]
    rest_rows = rest.reshape(2, -1, width)
    tile = size // 2
    groups = blocks * size // LANES
    rest_steps = rest_rows.shape[1] // tile
    steps = rest_steps + last.shape[1] // tile
    flat = rhs.reshape(-1, LANES)
    out = pl.pallas_call(
        functools.partial(update_kernel, rest_steps),
        grid=(steps,),
        out_shape=jax.ShapeDtypeStruct(flat.shape, flat.dtype),
        in_specs=[
            pl.BlockSpec((2, tile, width), lambda i: (0, jnp.minimum(i, rest_steps - 1), 0)),
            pl.BlockSpec((2, tile, width), lambda i: (0, jnp.maximum(i - rest_steps, 0), 0)),
            pl.BlockSpec(cols.shape, lambda i: (0, 0, 0, 0)),
            pl.BlockSpec(x.shape, lambda i: (0, 0, 0)),
            pl.BlockSpec((tile * groups, LANES), lambda i: (i, 0)),
        ],
        out_specs=pl.BlockSpec((tile * groups, LANES), lambda i: (i, 0)),
        scratch_shapes=[
            pltpu.VMEM((2, size, size), jnp.bfloat16),
            pltpu.VMEM((size, size), jnp.bfloat16),
            pltpu.VMEM((blocks, size, width), jnp.bfloat16),
        ],
        compiler_params=pltpu.CompilerParams(vmem_limit_bytes=VMEM_LIMIT),
    )(rest_rows, last, cols, x, flat)
    return out.reshape(rhs.shape)


def on_device(rhs, panels, inverses):
    row_index = lax.axis_index("row")
    col_index = lax.axis_index("col")
    row_count = lax.axis_size("row")
    col_count = lax.axis_size("col")
    blocks_here = panels.shape[1]
    col_blocks = rhs.shape[3]
    size = rhs.shape[-1]
    last = lax.all_gather(panels[:, blocks_here - 1, 0], "col", axis=1, tiled=True)
    rest_here, last = lax.optimization_barrier((panels[:, : blocks_here - 1, 0], last))
    rest = lax.all_gather(rest_here, "col", axis=2, tiled=True)
    rhs_last = rhs[blocks_here - 1, 0, :, col_blocks - 1, 0, :]
    upper, lower, g = share_corner(last, rhs_last, row_count, col_count)
    x = solve(upper, lower, g, inverses)
    chosen = []
    for b in range(col_blocks):
        place = col_index // row_count + b * (col_count // row_count)
        from_rest = lax.dynamic_index_in_dim(
            rest, jnp.minimum(place, blocks_here - 2), 1, False
        )
        chosen.append(jnp.where(place == blocks_here - 1, last, from_rest))
    cols = share_columns(jnp.stack(chosen, 1), row_count)
    new_rhs = update(rest, last, cols, x, rhs)
    rows_part = size // row_count
    cols_part = size // col_count
    solved = lax.dynamic_slice(
        x, (0, row_index * rows_part, col_index * cols_part), (2, rows_part, cols_part)
    )
    return (new_rhs, solved)


def solution(mesh):
    in_specs = (P(None, "row", None, None, "col", None), P(None, None, "row", "col", None), P())
    out_specs = (P(None, "row", None, None, "col", None), P(None, "row", "col"))
    return jax.shard_map(
        on_device, mesh=mesh, in_specs=in_specs, out_specs=out_specs, check_vma=False
    )
```

```python
import functools

import jax
import jax.numpy as jnp
from jax import lax
from jax.experimental import pallas as pl
from jax.experimental.pallas import tpu as pltpu
from jax.sharding import PartitionSpec as P

SWEEPS = 3
LANES = 128
MESH = pl.DeviceIdType.MESH
WINDOW = 2
VMEM_LIMIT = 50 * 1024 * 1024


def remote(src, dst, send_sem, recv_sem, row, col):
    return pltpu.make_async_remote_copy(
        src_ref=src, dst_ref=dst, send_sem=send_sem, recv_sem=recv_sem,
        device_id=(row, col), device_id_type=MESH,
    )


def greet(partners):
    barrier = pltpu.get_barrier_semaphore()
    for row, col in partners:
        pl.semaphore_signal(barrier, inc=1, device_id=(row, col), device_id_type=MESH)
    pl.semaphore_wait(barrier, len(partners))


def other_rows_of(row, row_count):
    return [lax.rem(row + j, row_count) for j in range(1, row_count)]


def g_kernel(
    row_count, col_count, g_ref, g_out,
    send_g1, send_g2, send_g3, send_g4, recv_g1, recv_g2, recv_g3, recv_g4, local_sem,
):
    row = lax.axis_index("row")
    col = lax.axis_index("col")
    core = lax.rem(col, 2)
    sibling = col + 1 - 2 * core
    part = g_ref.shape[0] // row_count
    last_col = col_count - 1
    other_rows = other_rows_of(row, row_count)
    other_cols = [lax.rem(col + 2 * j, col_count) for j in range(1, col_count // 2)]
    greet([(r, col) for r in other_rows] + [(row, c) for c in other_cols] + [(row, sibling)])

    def rows_of(index):
        return pl.ds(pl.multiple_of(index * part, part), part)

    mine = rows_of(row)
    g_mine = g_out.at[:, mine, :]
    sources = ((row_count - 2, 0), (row_count - 1, 1))

    @pl.when(col == last_col)
    def _():
        for source_row, slot in sources:

            @pl.when(row == source_row)
            def _():
                pltpu.make_async_copy(
                    g_ref.at[mine, :], g_out.at[slot, mine, :], local_sem.at[slot]
                ).start()
                for j, r in enumerate(other_rows):
                    theirs = rows_of(r)
                    remote(
                        g_ref.at[theirs, :], g_out.at[slot, theirs, :],
                        send_g1.at[slot, j], recv_g1.at[slot], r, col,
                    ).start()

        for source_row, slot in sources:
            piece = g_out.at[slot, mine, :]

            @pl.when(row == source_row)
            def _():
                pltpu.make_async_copy(g_ref.at[mine, :], piece, local_sem.at[slot]).wait()

            @pl.when(row != source_row)
            def _():
                remote(piece, piece, send_g1.at[slot, 0], recv_g1.at[slot], row, col).wait_recv()

        for j, c in enumerate(other_cols):
            remote(g_mine, g_mine, send_g2.at[j], recv_g2, row, c).start()

    @pl.when(core == 1)
    def _():
        @pl.when(col != last_col)
        def _():
            remote(g_mine, g_mine, send_g2.at[0], recv_g2, row, col).wait_recv()

        for j, r in enumerate(other_rows):
            remote(g_mine, g_mine, send_g3.at[j], recv_g3.at[row], r, col).start()
        remote(g_mine, g_mine, send_g4.at[row], recv_g4.at[row], row, sibling).start()
        for r in other_rows:
            piece = g_out.at[:, rows_of(r), :]
            remote(piece, piece, send_g3.at[0], recv_g3.at[r], row, col).wait_recv()
            remote(piece, piece, send_g4.at[r], recv_g4.at[r], row, sibling).start()

    for r in [row] + other_rows:
        piece = g_out.at[:, rows_of(r), :]

        @pl.when(core == 0)
        def _():
            remote(piece, piece, send_g4.at[r], recv_g4.at[r], row, sibling).wait_recv()

        @pl.when(core == 1)
        def _():
            remote(piece, piece, send_g4.at[r], recv_g4.at[r], row, sibling).wait_send()

    @pl.when(core == 1)
    def _():
        for j, r in enumerate(other_rows):
            remote(g_mine, g_mine, send_g3.at[j], recv_g3.at[row], r, col).wait_send()

    @pl.when(col == last_col)
    def _():
        for source_row, slot in sources:

            @pl.when(row == source_row)
            def _():
                for j, r in enumerate(other_rows):
                    theirs = rows_of(r)
                    remote(
                        g_ref.at[theirs, :], g_out.at[slot, theirs, :],
                        send_g1.at[slot, j], recv_g1.at[slot], r, col,
                    ).wait_send()

        for j, c in enumerate(other_cols):
            remote(g_mine, g_mine, send_g2.at[j], recv_g2, row, c).wait_send()


def share_g(rhs_last, row_count, col_count):
    size = rhs_last.shape[0]
    dma = pltpu.SemaphoreType.DMA
    peers = row_count - 1
    return pl.pallas_call(
        functools.partial(g_kernel, row_count, col_count),
        out_shape=jax.ShapeDtypeStruct((2, size, size), jnp.float32),
        in_specs=[pl.BlockSpec(memory_space=pl.ANY)],
        out_specs=pl.BlockSpec(memory_space=pl.ANY),
        scratch_shapes=[
            dma((2, peers)), dma((col_count // 2,)), dma((peers,)), dma((row_count,)),
            dma((2,)), dma, dma((row_count,)), dma((row_count,)), dma((2,)),
        ],
        compiler_params=pltpu.CompilerParams(collective_id=0, has_side_effects=True),
        cost_estimate=pl.CostEstimate(flops=0, bytes_accessed=60_000_000, transcendentals=0),
    )(rhs_last)


def chain_of(row, source, backward, row_count):
    place = jnp.int32(0)
    after = jnp.int32(0)
    for s in range(row_count):
        forward = [s ^ (i ^ (i >> 1)) for i in range(row_count)]
        for b, order in enumerate((forward, forward[:1] + forward[:0:-1])):
            for i, r in enumerate(order):
                hit = jnp.logical_and(jnp.logical_and(source == s, backward == b), row == r)
                place = jnp.where(hit, i, place)
                after = jnp.where(hit, order[(i + 1) % row_count], after)
    return place, after


def run_chains(chains, row, col, row_count, on_arrival):
    for n in range(max(len(chain[2]) for chain in chains)):
        for which, (place, after, chunks, send, recv) in enumerate(chains):
            if n >= len(chunks):
                continue
            src, dst = chunks[n]

            @pl.when(place == 0)
            def _():
                if n >= WINDOW:
                    old_src, old_dst = chunks[n - WINDOW]
                    remote(
                        old_src, old_dst, send.at[n - WINDOW], recv.at[n - WINDOW], after, col
                    ).wait_send()
                remote(src, dst, send.at[n], recv.at[n], after, col).start()

            @pl.when(place > 0)
            def _():
                remote(dst, dst, send.at[n], recv.at[n], after, col).wait_recv()

                @pl.when(place < row_count - 1)
                def _():
                    remote(dst, dst, send.at[n], recv.at[n], after, col).start()

                on_arrival(which, n)

    for place, after, chunks, send, recv in chains:
        for n, (src, dst) in enumerate(chunks):
            waits = place < row_count - 1
            if n < len(chunks) - WINDOW:
                waits = jnp.logical_and(waits, place > 0)

            @pl.when(waits)
            def _():
                remote(dst, dst, send.at[n], recv.at[n], after, col).wait_send()


def corner_kernel(
    row_count, last_ref, upper, lower,
    send_upper, recv_upper, send_lower, recv_lower,
    sib_send_upper, sib_recv_upper, sib_send_lower, sib_recv_lower, local_sem,
):
    row = lax.axis_index("row")
    col = lax.axis_index("col")
    core = lax.rem(col, 2)
    sibling = col + 1 - 2 * core
    size = last_ref.shape[1]
    half = size // 2
    part = half // 4
    greet([(r, col) for r in other_rows_of(row, row_count)] + [(row, sibling)])

    own_copies = (
        (row_count - 2, last_ref, upper, local_sem.at[0]),
        (row_count - 1, last_ref.at[:, :, pl.ds(size, size)], lower, local_sem.at[1]),
    )
    for source_row, src, out, sem in own_copies:

        @pl.when(row == source_row)
        def _():
            pltpu.make_async_copy(src, out, sem).start()

    def rows_at(which_half, p):
        return pl.ds(pl.multiple_of(which_half * half + p * part, part), part)

    chains = []
    siblings = []
    for source_row, src, out, sends in (
        (row_count - 2, last_ref, upper, (send_upper, recv_upper, sib_send_upper, sib_recv_upper)),
        (row_count - 1, last_ref.at[:, :, pl.ds(size, size)], lower,
         (send_lower, recv_lower, sib_send_lower, sib_recv_lower)),
    ):
        place, after = chain_of(row, source_row, core, row_count)
        pieces = [(m, p) for p in range(4) for m in range(2)]
        chunks = [
            (src.at[m, rows_at(core, p), :], out.at[m, rows_at(core, p), :]) for m, p in pieces
        ]
        arriving = [out.at[m, rows_at(1 - core, p), :] for m, p in pieces]
        chains.append((place, after, chunks, sends[0], sends[1]))
        siblings.append((place, arriving, sends[2], sends[3]))

    def to_sibling(which, n):
        dst = chains[which][2][n][1]
        _, _, send, recv = siblings[which]
        remote(dst, dst, send.at[n], recv.at[n], row, sibling).start()

    run_chains(chains, row, col, row_count, to_sibling)

    for which, (place, arriving, send, recv) in enumerate(siblings):

        @pl.when(place > 0)
        def _():
            for n, ref in enumerate(arriving):
                dst = chains[which][2][n][1]
                remote(ref, ref, send.at[n], recv.at[n], row, sibling).wait_recv()
                remote(dst, dst, send.at[n], recv.at[n], row, sibling).wait_send()

    for source_row, src, out, sem in own_copies:

        @pl.when(row == source_row)
        def _():
            pltpu.make_async_copy(src, out, sem).wait()


def share_corner(last_rows, row_count):
    _, size, width = last_rows.shape
    dma = pltpu.SemaphoreType.DMA
    return pl.pallas_call(
        functools.partial(corner_kernel, row_count),
        out_shape=(
            jax.ShapeDtypeStruct((2, size, width), jnp.bfloat16),
            jax.ShapeDtypeStruct((2, size, size), jnp.bfloat16),
        ),
        in_specs=[pl.BlockSpec(memory_space=pl.ANY)],
        out_specs=[pl.BlockSpec(memory_space=pl.ANY)] * 2,
        scratch_shapes=[dma((8,))] * 8 + [dma((2,))],
        compiler_params=pltpu.CompilerParams(collective_id=2, has_side_effects=True),
        cost_estimate=pl.CostEstimate(flops=0, bytes_accessed=60_000_000, transcendentals=0),
    )(last_rows)


def mm(left, right):
    return lax.dot_general(left, right, (((1,), (0,)), ((), ())), preferred_element_type=jnp.float32)


def mm_t(left, right):
    return lax.dot_general(left, right, (((1,), (1,)), ((), ())), preferred_element_type=jnp.float32)


def split(value):
    high = value.astype(jnp.bfloat16)
    low = (value - high.astype(jnp.float32)).astype(jnp.bfloat16)
    return high, low


def upper_times(tri, parts):
    half = tri[0].shape[0] // 2
    top = bottom = None
    for i, t in enumerate(tri):
        for j, p in enumerate(parts):
            if i + j < 2:
                a = mm(t[:half], p)
                b = mm(t[half:, half:], p[half:])
                top = a if top is None else top + a
                bottom = b if bottom is None else bottom + b
    return jnp.concatenate([top, bottom], 0)


def times_upper_t(parts, tri):
    half = tri[0].shape[0] // 2
    left = right = None
    for i, t in enumerate(tri):
        for j, p in enumerate(parts):
            if i + j < 2:
                a = mm_t(p, t[:half])
                b = mm_t(p[:, half:], t[half:, half:])
                left = a if left is None else left + a
                right = b if right is None else right + b
    return jnp.concatenate([left, right], 1)


def solve_kernel(upper, lower, g, inverses, out, inv_high, inv_low):
    size = g.shape[1]
    for i in range(3):
        high, low = split(inverses[i])
        inv_high[i] = high
        inv_low[i] = low

    def precondition(i, residual):
        first = upper_times((inv_high[i], inv_low[i]), split(residual))
        return times_upper_t(split(first), (inv_high[2], inv_low[2]))

    def corner_update(residual):
        update = precondition(1, residual)
        return 0.25 * (update + update.T)

    out[0] = corner_update(-g[1])

    def corner_sweep(_, carry):
        first = upper_times((lower[0],), split(out[0]))
        term = times_upper_t(split(first), (lower[1],))
        out[0] = out[0] + corner_update(-g[1] - (term + term.T))
        return carry

    lax.fori_loop(1, SWEEPS, corner_sweep, 0)

    parts = split(out[0])
    over_a = split(sum(mm(upper[0, :, size:], p) for p in parts))
    over_e = split(sum(mm(upper[1, :, size:], p) for p in parts))
    g[0] = -g[0] - (times_upper_t(over_a, (lower[1],)) + times_upper_t(over_e, (lower[0],)))
    out[1] = 0.5 * precondition(0, g[0])

    def upper_sweep(_, carry):
        held = split(out[1])
        by_a = split(upper_times((upper[0, :, :size],), held))
        by_e = split(upper_times((upper[1, :, :size],), held))
        term = times_upper_t(by_a, (lower[1],)) + times_upper_t(by_e, (lower[0],))
        out[1] = out[1] + 0.5 * precondition(0, g[0] - term)
        return carry

    lax.fori_loop(1, SWEEPS, upper_sweep, 0)


def solve(upper, lower, g, inverses):
    size = g.shape[1]
    return pl.pallas_call(
        solve_kernel,
        out_shape=jax.ShapeDtypeStruct((2, size, size), jnp.float32),
        in_specs=[pl.BlockSpec(memory_space=pltpu.VMEM)] * 4,
        out_specs=pl.BlockSpec(memory_space=pltpu.VMEM),
        scratch_shapes=[
            pltpu.VMEM((3, size, size), jnp.bfloat16),
            pltpu.VMEM((3, size, size), jnp.bfloat16),
        ],
        compiler_params=pltpu.CompilerParams(vmem_limit_bytes=VMEM_LIMIT),
        cost_estimate=pl.CostEstimate(
            flops=100 * size ** 3, bytes_accessed=100_000_000, transcendentals=0
        ),
    )(upper, lower, g, inverses)


def column_kernel(row_count, chosen, out, send, recv, local_sem):
    row = lax.axis_index("row")
    col = lax.axis_index("col")
    matrices, blocks, size, _ = chosen.shape
    part = size // 4
    greet([(r, col) for r in other_rows_of(row, row_count)])
    place, after = chain_of(row, lax.rem(col, row_count), 0, row_count)

    @pl.when(place == 0)
    def _():
        pltpu.make_async_copy(chosen, out, local_sem).start()

    chunks = []
    for b in range(blocks):
        for p in range(4):
            for m in range(matrices):
                rows = pl.ds(p * part, part)
                chunks.append((chosen.at[m, b, rows, :], out.at[m, b, rows, :]))
    run_chains([(place, after, chunks, send, recv)], row, col, row_count, lambda which, n: None)

    @pl.when(place == 0)
    def _():
        pltpu.make_async_copy(chosen, out, local_sem).wait()


def share_columns(chosen, row_count):
    count = chosen.shape[0] * chosen.shape[1] * 4
    dma = pltpu.SemaphoreType.DMA
    return pl.pallas_call(
        functools.partial(column_kernel, row_count),
        out_shape=jax.ShapeDtypeStruct(chosen.shape, chosen.dtype),
        in_specs=[pl.BlockSpec(memory_space=pl.ANY)],
        out_specs=pl.BlockSpec(memory_space=pl.ANY),
        scratch_shapes=[dma((count,)), dma((count,)), dma],
        compiler_params=pltpu.CompilerParams(collective_id=1, has_side_effects=True),
        cost_estimate=pl.CostEstimate(flops=0, bytes_accessed=60_000_000, transcendentals=0),
    )(chosen)


def update_kernel(
    rest_steps, rest_ref, last_ref, cols_ref, x_ref, rhs_ref, out_ref, x_high, x_turned, z_cols
):
    step = pl.program_id(0)
    size = x_ref.shape[1]
    tile = rest_ref.shape[1]
    groups = rhs_ref.shape[0] // tile

    def times_known(left):
        from_right = left[:, size:]
        first = mm(from_right, x_turned[...])
        second = mm(left[:, :size], x_high[1]) + mm(from_right, x_high[0])
        return jnp.concatenate([first, second], 1).astype(jnp.bfloat16)

    @pl.when(step == 0)
    def _():
        x_high[...] = x_ref[...].astype(jnp.bfloat16)
        x_turned[...] = x_ref[1].T.astype(jnp.bfloat16)
        for b in range(z_cols.shape[0]):
            z_cols[b] = times_known(cols_ref[0, b])

    def work(rows_ref):
        z_rows = times_known(rows_ref[0])
        for b in range(z_cols.shape[0]):
            total = mm_t(z_rows, cols_ref[1, b]) + mm_t(rows_ref[1], z_cols[b])
            for q in range(size // LANES):
                where = pl.ds(b * (size // LANES) + q, tile, stride=groups)
                out_ref[where, :] = rhs_ref[where, :] + total[:, q * LANES:(q + 1) * LANES]

    @pl.when(step < rest_steps)
    def _():
        work(rest_ref)

    @pl.when(step >= rest_steps)
    def _():
        work(last_ref)


def update(rest, last, cols, x, rhs):
    size = x.shape[1]
    width = rest.shape[-1]
    blocks = cols.shape[1]
    rest_rows = rest.reshape(2, -1, width)
    tile = size // 2
    groups = blocks * size // LANES
    rest_steps = rest_rows.shape[1] // tile
    steps = rest_steps + last.shape[1] // tile
    flat = rhs.reshape(-1, LANES)
    out = pl.pallas_call(
        functools.partial(update_kernel, rest_steps),
        grid=(steps,),
        out_shape=jax.ShapeDtypeStruct(flat.shape, flat.dtype),
        in_specs=[
            pl.BlockSpec((2, tile, width), lambda i: (0, jnp.minimum(i, rest_steps - 1), 0)),
            pl.BlockSpec((2, tile, width), lambda i: (0, jnp.maximum(i - rest_steps, 0), 0)),
            pl.BlockSpec(cols.shape, lambda i: (0, 0, 0, 0)),
            pl.BlockSpec(x.shape, lambda i: (0, 0, 0)),
            pl.BlockSpec((tile * groups, LANES), lambda i: (i, 0)),
        ],
        out_specs=pl.BlockSpec((tile * groups, LANES), lambda i: (i, 0)),
        scratch_shapes=[
            pltpu.VMEM((2, size, size), jnp.bfloat16),
            pltpu.VMEM((size, size), jnp.bfloat16),
            pltpu.VMEM((blocks, size, width), jnp.bfloat16),
        ],
        compiler_params=pltpu.CompilerParams(vmem_limit_bytes=VMEM_LIMIT),
    )(rest_rows, last, cols, x, flat)
    return out.reshape(rhs.shape)


def on_device(rhs, panels, inverses):
    row_index = lax.axis_index("row")
    col_index = lax.axis_index("col")
    row_count = lax.axis_size("row")
    col_count = lax.axis_size("col")
    blocks_here = panels.shape[1]
    col_blocks = rhs.shape[3]
    size = rhs.shape[-1]
    last = lax.all_gather(panels[:, blocks_here - 1, 0], "col", axis=1, tiled=True)
    rhs_last = rhs[blocks_here - 1, 0, :, col_blocks - 1, 0, :]
    g = share_g(rhs_last, row_count, col_count)
    rest_here, last, g = lax.optimization_barrier((panels[:, : blocks_here - 1, 0], last, g))
    rest = lax.all_gather(rest_here, "col", axis=2, tiled=True)
    upper, lower = share_corner(last, row_count)
    x = solve(upper, lower, g, inverses)
    chosen = []
    for b in range(col_blocks):
        place = col_index // row_count + b * (col_count // row_count)
        from_rest = lax.dynamic_index_in_dim(
            rest, jnp.minimum(place, blocks_here - 2), 1, False
        )
        chosen.append(jnp.where(place == blocks_here - 1, last, from_rest))
    cols = share_columns(jnp.stack(chosen, 1), row_count)
    new_rhs = update(rest, last, cols, x, rhs)
    rows_part = size // row_count
    cols_part = size // col_count
    solved = lax.dynamic_slice(
        x, (0, row_index * rows_part, col_index * cols_part), (2, rows_part, cols_part)
    )
    return (new_rhs, solved)


def solution(mesh):
    in_specs = (P(None, "row", None, None, "col", None), P(None, None, "row", "col", None), P())
    out_specs = (P(None, "row", None, None, "col", None), P(None, "row", "col"))
    return jax.shard_map(
        on_device, mesh=mesh, in_specs=in_specs, out_specs=out_specs, check_vma=False
    )
```

```python
import functools

import jax
import jax.numpy as jnp
from jax import lax
from jax.experimental import pallas as pl
from jax.experimental.pallas import tpu as pltpu
from jax.sharding import PartitionSpec as P

SWEEPS = 3
LANES = 128
MESH = pl.DeviceIdType.MESH
CORNER_PARTS = 4
COLUMN_PARTS = 4
VMEM_LIMIT = 50 * 1024 * 1024


def remote(src, dst, send_sem, recv_sem, row, col):
    return pltpu.make_async_remote_copy(
        src_ref=src, dst_ref=dst, send_sem=send_sem, recv_sem=recv_sem,
        device_id=(row, col), device_id_type=MESH,
    )


def greet(partners):
    barrier = pltpu.get_barrier_semaphore()
    for row, col in partners:
        pl.semaphore_signal(barrier, inc=1, device_id=(row, col), device_id_type=MESH)
    pl.semaphore_wait(barrier, len(partners))


def other_rows_of(row, row_count):
    return [lax.rem(row + j, row_count) for j in range(1, row_count)]


def g_kernel(
    row_count, col_count, g_ref, g_out,
    send_first, send_line, send_rows, send_sibling,
    recv_first, recv_line, recv_rows, recv_sibling, local_sem,
):
    row = lax.axis_index("row")
    col = lax.axis_index("col")
    core = lax.rem(col, 2)
    sibling = col + 1 - 2 * core
    part = g_ref.shape[0] // (2 * row_count)
    last_col = col_count - 1
    other_rows = other_rows_of(row, row_count)
    other_cols = [lax.rem(col + 2 * j, col_count) for j in range(1, col_count // 2)]
    on_last_chip = col >= last_col - 1
    greet(
        [(r, col) for r in other_rows]
        + [(r, sibling) for r in other_rows]
        + [(row, c) for c in other_cols]
        + [(row, sibling)]
    )

    def rows_of(r, k):
        return pl.ds(pl.multiple_of((2 * r + k) * part, part), part)

    mine = rows_of(row, core)
    g_mine = g_out.at[:, mine, :]
    sources = ((row_count - 2, 0), (row_count - 1, 1))

    def first_sends(slot):
        for j, (r, k) in enumerate(
            [(r, k) for r in other_rows for k in range(2)] + [(row, 0)]
        ):
            theirs = rows_of(r, k)
            yield remote(
                g_ref.at[theirs, :], g_out.at[slot, theirs, :],
                send_first.at[slot, j], recv_first.at[slot], r, last_col - 1 + k,
            )

    @pl.when(on_last_chip)
    def _():
        for source_row, slot in sources:

            @pl.when(jnp.logical_and(row == source_row, col == last_col))
            def _():
                pltpu.make_async_copy(
                    g_ref.at[mine, :], g_out.at[slot, mine, :], local_sem.at[slot]
                ).start()
                for copy in first_sends(slot):
                    copy.start()

        for source_row, slot in sources:
            piece = g_out.at[slot, mine, :]
            holder = jnp.logical_and(row == source_row, col == last_col)

            @pl.when(holder)
            def _():
                pltpu.make_async_copy(g_ref.at[mine, :], piece, local_sem.at[slot]).wait()

            @pl.when(jnp.logical_not(holder))
            def _():
                remote(piece, piece, send_first.at[slot, 0], recv_first.at[slot], row, col).wait_recv()

        for j, c in enumerate(other_cols):
            remote(g_mine, g_mine, send_line.at[j], recv_line, row, c).start()

    @pl.when(jnp.logical_not(on_last_chip))
    def _():
        remote(g_mine, g_mine, send_line.at[0], recv_line, row, col).wait_recv()

    for j, r in enumerate(other_rows):
        remote(g_mine, g_mine, send_rows.at[j], recv_rows.at[row], r, col).start()
    remote(g_mine, g_mine, send_sibling.at[row], recv_sibling.at[row], row, sibling).start()
    for r in other_rows:
        piece = g_out.at[:, rows_of(r, core), :]
        remote(piece, piece, send_rows.at[0], recv_rows.at[r], row, col).wait_recv()
        remote(piece, piece, send_sibling.at[r], recv_sibling.at[r], row, sibling).start()
    for r in [row] + other_rows:
        piece = g_out.at[:, rows_of(r, 1 - core), :]
        remote(piece, piece, send_sibling.at[r], recv_sibling.at[r], row, sibling).wait_recv()
        remote(piece, piece, send_sibling.at[r], recv_sibling.at[r], row, sibling).wait_send()
    for j, r in enumerate(other_rows):
        remote(g_mine, g_mine, send_rows.at[j], recv_rows.at[row], r, col).wait_send()

    @pl.when(on_last_chip)
    def _():
        for source_row, slot in sources:

            @pl.when(jnp.logical_and(row == source_row, col == last_col))
            def _():
                for copy in first_sends(slot):
                    copy.wait_send()

        for j, c in enumerate(other_cols):
            remote(g_mine, g_mine, send_line.at[j], recv_line, row, c).wait_send()


def share_g(rhs_last, row_count, col_count):
    size = rhs_last.shape[0]
    dma = pltpu.SemaphoreType.DMA
    peers = row_count - 1
    return pl.pallas_call(
        functools.partial(g_kernel, row_count, col_count),
        out_shape=jax.ShapeDtypeStruct((2, size, size), jnp.float32),
        in_specs=[pl.BlockSpec(memory_space=pl.ANY)],
        out_specs=pl.BlockSpec(memory_space=pl.ANY),
        scratch_shapes=[
            dma((2, 2 * peers + 1)), dma((col_count // 2,)), dma((peers,)), dma((row_count,)),
            dma((2,)), dma, dma((row_count,)), dma((row_count,)), dma((2,)),
        ],
        compiler_params=pltpu.CompilerParams(collective_id=0, has_side_effects=True),
        cost_estimate=pl.CostEstimate(flops=0, bytes_accessed=60_000_000, transcendentals=0),
    )(rhs_last)


def chain_of(row, source, backward, row_count):
    place = jnp.int32(0)
    after = jnp.int32(0)
    for s in range(row_count):
        forward = [s ^ (i ^ (i >> 1)) for i in range(row_count)]
        for b, order in enumerate((forward, forward[:1] + forward[:0:-1])):
            for i, r in enumerate(order):
                hit = jnp.logical_and(jnp.logical_and(source == s, backward == b), row == r)
                place = jnp.where(hit, i, place)
                after = jnp.where(hit, order[(i + 1) % row_count], after)
    return place, after


def run_chains(chains, row, col, row_count, on_arrival):
    for n in range(len(chains[0][3])):
        for place, after, start, landings, send, recv in chains:

            @pl.when(place == 0)
            def _():
                start(n, after)

    for n in range(len(chains[0][3])):
        for which, (place, after, start, landings, send, recv) in enumerate(chains):
            dst = landings[n]

            @pl.when(place > 0)
            def _():
                remote(dst, dst, send.at[n], recv.at[n], after, col).wait_recv()

                @pl.when(place < row_count - 1)
                def _():
                    remote(dst, dst, send.at[n], recv.at[n], after, col).start()

                on_arrival(which, n)

    for place, after, start, landings, send, recv in chains:

        @pl.when(place < row_count - 1)
        def _():
            for n, dst in enumerate(landings):
                remote(dst, dst, send.at[n], recv.at[n], after, col).wait_send()


def corner_kernel(
    row_count, last_ref, upper, lower, send, recv, sibling_send, sibling_recv, local_sem
):
    row = lax.axis_index("row")
    col = lax.axis_index("col")
    core = lax.rem(col, 2)
    sibling = col + 1 - 2 * core
    size = last_ref.shape[1]
    half = size // 2
    part = half // CORNER_PARTS
    greet([(r, col) for r in other_rows_of(row, row_count)] + [(row, sibling)])
    sources = (
        (row_count - 2, last_ref, upper),
        (row_count - 1, last_ref.at[:, :, pl.ds(size, size)], lower),
    )
    for slot, (source_row, src, out) in enumerate(sources):

        @pl.when(row == source_row)
        def _():
            pltpu.make_async_copy(src, out, local_sem.at[slot]).start()

    def rows_at(which_half, p):
        return pl.ds(pl.multiple_of(which_half * half + p * part, part), part)

    chains = []
    arriving = []
    for slot, (source_row, src, out) in enumerate(sources):
        for way in range(2):
            index = 2 * slot + way
            place, after = chain_of(row, source_row, way, row_count)

            def start(n, to, index=index, way=way, src=src, out=out):
                rows = rows_at(core, n)
                remote(
                    src.at[way, rows, :], out.at[way, rows, :],
                    send.at[index, n], recv.at[index, n], to, col,
                ).start()

            landings = [out.at[way, rows_at(core, n), :] for n in range(CORNER_PARTS)]
            arriving.append([out.at[way, rows_at(1 - core, n), :] for n in range(CORNER_PARTS)])
            chains.append((place, after, start, landings, send.at[index], recv.at[index]))

    def to_sibling(which, n):
        dst = chains[which][3][n]
        remote(dst, dst, sibling_send.at[which, n], sibling_recv.at[which, n], row, sibling).start()

    run_chains(chains, row, col, row_count, to_sibling)

    for which, chain in enumerate(chains):

        @pl.when(chain[0] > 0)
        def _():
            for n, ref in enumerate(arriving[which]):
                done = remote(
                    ref, ref, sibling_send.at[which, n], sibling_recv.at[which, n], row, sibling
                )
                done.wait_recv()
                done.wait_send()

    for slot, (source_row, src, out) in enumerate(sources):

        @pl.when(row == source_row)
        def _():
            pltpu.make_async_copy(src, out, local_sem.at[slot]).wait()


def share_corner(last_rows, row_count):
    _, size, width = last_rows.shape
    dma = pltpu.SemaphoreType.DMA
    return pl.pallas_call(
        functools.partial(corner_kernel, row_count),
        out_shape=(
            jax.ShapeDtypeStruct((2, size, width), jnp.bfloat16),
            jax.ShapeDtypeStruct((2, size, size), jnp.bfloat16),
        ),
        in_specs=[pl.BlockSpec(memory_space=pl.ANY)],
        out_specs=[pl.BlockSpec(memory_space=pl.ANY)] * 2,
        scratch_shapes=[dma((4, CORNER_PARTS))] * 4 + [dma((2,))],
        compiler_params=pltpu.CompilerParams(collective_id=2, has_side_effects=True),
        cost_estimate=pl.CostEstimate(flops=0, bytes_accessed=60_000_000, transcendentals=0),
    )(last_rows)


def mm(left, right):
    return lax.dot_general(left, right, (((1,), (0,)), ((), ())), preferred_element_type=jnp.float32)


def mm_t(left, right):
    return lax.dot_general(left, right, (((1,), (1,)), ((), ())), preferred_element_type=jnp.float32)


def split(value):
    high = value.astype(jnp.bfloat16)
    low = (value - high.astype(jnp.float32)).astype(jnp.bfloat16)
    return high, low


def upper_times(tri, parts):
    half = tri[0].shape[0] // 2
    top = bottom = None
    for i, t in enumerate(tri):
        for j, p in enumerate(parts):
            if i + j < 2:
                a = mm(t[:half], p)
                b = mm(t[half:, half:], p[half:])
                top = a if top is None else top + a
                bottom = b if bottom is None else bottom + b
    return jnp.concatenate([top, bottom], 0)


def times_upper_t(parts, tri):
    half = tri[0].shape[0] // 2
    left = right = None
    for i, t in enumerate(tri):
        for j, p in enumerate(parts):
            if i + j < 2:
                a = mm_t(p, t[:half])
                b = mm_t(p[:, half:], t[half:, half:])
                left = a if left is None else left + a
                right = b if right is None else right + b
    return jnp.concatenate([left, right], 1)


def solve_kernel(upper, lower, g, inverses, out, inv_high, inv_low):
    size = g.shape[1]
    for i in range(3):
        high, low = split(inverses[i])
        inv_high[i] = high
        inv_low[i] = low

    def precondition(i, residual):
        first = upper_times((inv_high[i], inv_low[i]), split(residual))
        return times_upper_t(split(first), (inv_high[2], inv_low[2]))

    def corner_update(residual):
        update = precondition(1, residual)
        return 0.25 * (update + update.T)

    out[0] = corner_update(-g[1])

    def corner_sweep(_, carry):
        first = upper_times((lower[0],), split(out[0]))
        term = times_upper_t(split(first), (lower[1],))
        out[0] = out[0] + corner_update(-g[1] - (term + term.T))
        return carry

    lax.fori_loop(1, SWEEPS, corner_sweep, 0)

    parts = split(out[0])
    over_a = split(sum(mm(upper[0, :, size:], p) for p in parts))
    over_e = split(sum(mm(upper[1, :, size:], p) for p in parts))
    g[0] = -g[0] - (times_upper_t(over_a, (lower[1],)) + times_upper_t(over_e, (lower[0],)))
    out[1] = 0.5 * precondition(0, g[0])

    def upper_sweep(_, carry):
        held = split(out[1])
        by_a = split(upper_times((upper[0, :, :size],), held))
        by_e = split(upper_times((upper[1, :, :size],), held))
        term = times_upper_t(by_a, (lower[1],)) + times_upper_t(by_e, (lower[0],))
        out[1] = out[1] + 0.5 * precondition(0, g[0] - term)
        return carry

    lax.fori_loop(1, SWEEPS, upper_sweep, 0)


def solve(upper, lower, g, inverses):
    size = g.shape[1]
    return pl.pallas_call(
        solve_kernel,
        out_shape=jax.ShapeDtypeStruct((2, size, size), jnp.float32),
        in_specs=[pl.BlockSpec(memory_space=pltpu.VMEM)] * 4,
        out_specs=pl.BlockSpec(memory_space=pltpu.VMEM),
        scratch_shapes=[
            pltpu.VMEM((3, size, size), jnp.bfloat16),
            pltpu.VMEM((3, size, size), jnp.bfloat16),
        ],
        compiler_params=pltpu.CompilerParams(vmem_limit_bytes=VMEM_LIMIT),
        cost_estimate=pl.CostEstimate(
            flops=100 * size ** 3, bytes_accessed=100_000_000, transcendentals=0
        ),
    )(upper, lower, g, inverses)


def column_kernel(row_count, col_count, rest_ref, last_ref, out, send, recv, local_sem):
    row = lax.axis_index("row")
    col = lax.axis_index("col")
    matrices, blocks, size, _ = out.shape
    part = size // COLUMN_PARTS
    group = col_count // row_count
    last_block = rest_ref.shape[1]
    greet([(r, col) for r in other_rows_of(row, row_count)])
    source = lax.rem(col, row_count)

    def from_block(b, use):
        block = col // row_count + b * group
        if (b + 1) * group > last_block:

            @pl.when(block == last_block)
            def _():
                use(last_ref)

            @pl.when(block < last_block)
            def _():
                use(rest_ref.at[:, jnp.minimum(block, last_block - 1)])

        else:
            use(rest_ref.at[:, block])

    pieces = [(b, p) for b in range(blocks) for p in range(COLUMN_PARTS)]
    chains = []
    for way in range(2):
        place, after = chain_of(row, source, way, row_count)

        def start(n, to, way=way):
            b, p = pieces[n]
            rows = pl.ds(p * part, part)
            from_block(
                b,
                lambda src: remote(
                    src.at[way, rows, :], out.at[way, b, rows, :],
                    send.at[way, n], recv.at[way, n], to, col,
                ).start(),
            )

        landings = [out.at[way, b, pl.ds(p * part, part), :] for b, p in pieces]
        chains.append((place, after, start, landings, send.at[way], recv.at[way]))

    def own(b, act):
        from_block(b, lambda src: act(pltpu.make_async_copy(src, out.at[:, b], local_sem.at[b])))

    @pl.when(row == source)
    def _():
        for b in range(blocks):
            own(b, lambda copy: copy.start())

    run_chains(chains, row, col, row_count, lambda which, n: None)

    @pl.when(row == source)
    def _():
        for b in range(blocks):
            own(b, lambda copy: copy.wait())


def share_columns(rest, last, col_blocks, row_count, col_count):
    matrices, _, size, width = rest.shape
    dma = pltpu.SemaphoreType.DMA
    return pl.pallas_call(
        functools.partial(column_kernel, row_count, col_count),
        out_shape=jax.ShapeDtypeStruct((matrices, col_blocks, size, width), rest.dtype),
        in_specs=[pl.BlockSpec(memory_space=pl.ANY)] * 2,
        out_specs=pl.BlockSpec(memory_space=pl.ANY),
        scratch_shapes=[dma((2, col_blocks * COLUMN_PARTS))] * 2 + [dma((col_blocks,))],
        compiler_params=pltpu.CompilerParams(collective_id=1, has_side_effects=True),
        cost_estimate=pl.CostEstimate(flops=0, bytes_accessed=60_000_000, transcendentals=0),
    )(rest, last)


def update_kernel(
    rest_steps, rest_ref, last_ref, cols_ref, x_ref, rhs_ref, out_ref, x_high, x_turned, z_cols
):
    step = pl.program_id(0)
    size = x_ref.shape[1]
    tile = rest_ref.shape[1]
    groups = rhs_ref.shape[0] // tile

    def times_known(left):
        from_right = left[:, size:]
        first = mm(from_right, x_turned[...])
        second = mm(left[:, :size], x_high[1]) + mm(from_right, x_high[0])
        return jnp.concatenate([first, second], 1).astype(jnp.bfloat16)

    @pl.when(step == 0)
    def _():
        x_high[...] = x_ref[...].astype(jnp.bfloat16)
        x_turned[...] = x_ref[1].T.astype(jnp.bfloat16)
        for b in range(z_cols.shape[0]):
            z_cols[b] = times_known(cols_ref[0, b])

    def work(rows_ref):
        z_rows = times_known(rows_ref[0])
        for b in range(z_cols.shape[0]):
            total = mm_t(z_rows, cols_ref[1, b]) + mm_t(rows_ref[1], z_cols[b])
            for q in range(size // LANES):
                where = pl.ds(b * (size // LANES) + q, tile, stride=groups)
                out_ref[where, :] = rhs_ref[where, :] + total[:, q * LANES:(q + 1) * LANES]

    @pl.when(step < rest_steps)
    def _():
        work(rest_ref)

    @pl.when(step >= rest_steps)
    def _():
        work(last_ref)


def update(rest, last, cols, x, rhs):
    size = x.shape[1]
    width = rest.shape[-1]
    blocks = cols.shape[1]
    rest_rows = rest.reshape(2, -1, width)
    tile = size // 2
    groups = blocks * size // LANES
    rest_steps = rest_rows.shape[1] // tile
    steps = rest_steps + last.shape[1] // tile
    flat = rhs.reshape(-1, LANES)
    out = pl.pallas_call(
        functools.partial(update_kernel, rest_steps),
        grid=(steps,),
        out_shape=jax.ShapeDtypeStruct(flat.shape, flat.dtype),
        in_specs=[
            pl.BlockSpec((2, tile, width), lambda i: (0, jnp.minimum(i, rest_steps - 1), 0)),
            pl.BlockSpec((2, tile, width), lambda i: (0, jnp.maximum(i - rest_steps, 0), 0)),
            pl.BlockSpec(cols.shape, lambda i: (0, 0, 0, 0)),
            pl.BlockSpec(x.shape, lambda i: (0, 0, 0)),
            pl.BlockSpec((tile * groups, LANES), lambda i: (i, 0)),
        ],
        out_specs=pl.BlockSpec((tile * groups, LANES), lambda i: (i, 0)),
        scratch_shapes=[
            pltpu.VMEM((2, size, size), jnp.bfloat16),
            pltpu.VMEM((size, size), jnp.bfloat16),
            pltpu.VMEM((blocks, size, width), jnp.bfloat16),
        ],
        compiler_params=pltpu.CompilerParams(vmem_limit_bytes=VMEM_LIMIT),
    )(rest_rows, last, cols, x, flat)
    return out.reshape(rhs.shape)


def on_device(rhs, panels, inverses):
    row_index = lax.axis_index("row")
    col_index = lax.axis_index("col")
    row_count = lax.axis_size("row")
    col_count = lax.axis_size("col")
    blocks_here = panels.shape[1]
    col_blocks = rhs.shape[3]
    size = rhs.shape[-1]
    last = lax.all_gather(panels[:, blocks_here - 1, 0], "col", axis=1, tiled=True)
    rhs_last = rhs[blocks_here - 1, 0, :, col_blocks - 1, 0, :]
    g = share_g(rhs_last, row_count, col_count)
    rest_here, last, g = lax.optimization_barrier((panels[:, : blocks_here - 1, 0], last, g))
    rest = lax.all_gather(rest_here, "col", axis=2, tiled=True)
    upper, lower = share_corner(last, row_count)
    x = solve(upper, lower, g, inverses)
    cols = share_columns(rest, last, col_blocks, row_count, col_count)
    new_rhs = update(rest, last, cols, x, rhs)
    rows_part = size // row_count
    cols_part = size // col_count
    solved = lax.dynamic_slice(
        x, (0, row_index * rows_part, col_index * cols_part), (2, rows_part, cols_part)
    )
    return (new_rhs, solved)


def solution(mesh):
    in_specs = (P(None, "row", None, None, "col", None), P(None, None, "row", "col", None), P())
    out_specs = (P(None, "row", None, None, "col", None), P(None, "row", "col"))
    return jax.shard_map(
        on_device, mesh=mesh, in_specs=in_specs, out_specs=out_specs, check_vma=False
    )
```

```python
import functools

import jax
import jax.numpy as jnp
from jax import lax
from jax.experimental import pallas as pl
from jax.experimental.pallas import tpu as pltpu
from jax.sharding import PartitionSpec as P

SWEEPS = 3
LANES = 128
MESH = pl.DeviceIdType.MESH
CORNER_PARTS = 4
COLUMN_PARTS = 4
VMEM_LIMIT = 50 * 1024 * 1024


def remote(src, dst, send_sem, recv_sem, row, col):
    return pltpu.make_async_remote_copy(
        src_ref=src, dst_ref=dst, send_sem=send_sem, recv_sem=recv_sem,
        device_id=(row, col), device_id_type=MESH,
    )


def greet(partners):
    barrier = pltpu.get_barrier_semaphore()
    for row, col in partners:
        pl.semaphore_signal(barrier, inc=1, device_id=(row, col), device_id_type=MESH)
    pl.semaphore_wait(barrier, len(partners))


def other_rows_of(row, row_count):
    return [lax.rem(row + j, row_count) for j in range(1, row_count)]


def g_kernel(
    row_count, col_count, g_ref, g_out,
    send_first, send_line, send_rows, send_sibling,
    recv_first, recv_line, recv_rows, recv_sibling, local_sem,
):
    row = lax.axis_index("row")
    col = lax.axis_index("col")
    core = lax.rem(col, 2)
    sibling = col + 1 - 2 * core
    part = g_ref.shape[0] // (2 * row_count)
    last_col = col_count - 1
    other_rows = other_rows_of(row, row_count)
    other_cols = [lax.rem(col + 2 * j, col_count) for j in range(1, col_count // 2)]
    on_last_chip = col >= last_col - 1
    greet(
        [(r, col) for r in other_rows]
        + [(r, sibling) for r in other_rows]
        + [(row, c) for c in other_cols]
        + [(row, sibling)]
    )

    def rows_of(r, k):
        return pl.ds(pl.multiple_of((2 * r + k) * part, part), part)

    mine = rows_of(row, core)
    g_mine = g_out.at[:, mine, :]
    sources = ((row_count - 2, 0), (row_count - 1, 1))

    def first_sends(slot):
        for j, (r, k) in enumerate(
            [(r, k) for r in other_rows for k in range(2)] + [(row, 0)]
        ):
            theirs = rows_of(r, k)
            yield remote(
                g_ref.at[theirs, :], g_out.at[slot, theirs, :],
                send_first.at[slot, j], recv_first.at[slot], r, last_col - 1 + k,
            )

    @pl.when(on_last_chip)
    def _():
        for source_row, slot in sources:

            @pl.when(jnp.logical_and(row == source_row, col == last_col))
            def _():
                pltpu.make_async_copy(
                    g_ref.at[mine, :], g_out.at[slot, mine, :], local_sem.at[slot]
                ).start()
                for copy in first_sends(slot):
                    copy.start()

        for source_row, slot in sources:
            piece = g_out.at[slot, mine, :]
            holder = jnp.logical_and(row == source_row, col == last_col)

            @pl.when(holder)
            def _():
                pltpu.make_async_copy(g_ref.at[mine, :], piece, local_sem.at[slot]).wait()

            @pl.when(jnp.logical_not(holder))
            def _():
                remote(piece, piece, send_first.at[slot, 0], recv_first.at[slot], row, col).wait_recv()

        for j, c in enumerate(other_cols):
            remote(g_mine, g_mine, send_line.at[j], recv_line, row, c).start()

    @pl.when(jnp.logical_not(on_last_chip))
    def _():
        remote(g_mine, g_mine, send_line.at[0], recv_line, row, col).wait_recv()

    for j, r in enumerate(other_rows):
        remote(g_mine, g_mine, send_rows.at[j], recv_rows.at[row], r, col).start()
    remote(g_mine, g_mine, send_sibling.at[row], recv_sibling.at[row], row, sibling).start()
    for r in other_rows:
        piece = g_out.at[:, rows_of(r, core), :]
        remote(piece, piece, send_rows.at[0], recv_rows.at[r], row, col).wait_recv()
        remote(piece, piece, send_sibling.at[r], recv_sibling.at[r], row, sibling).start()
    for r in [row] + other_rows:
        piece = g_out.at[:, rows_of(r, 1 - core), :]
        remote(piece, piece, send_sibling.at[r], recv_sibling.at[r], row, sibling).wait_recv()
        remote(piece, piece, send_sibling.at[r], recv_sibling.at[r], row, sibling).wait_send()
    for j, r in enumerate(other_rows):
        remote(g_mine, g_mine, send_rows.at[j], recv_rows.at[row], r, col).wait_send()

    @pl.when(on_last_chip)
    def _():
        for source_row, slot in sources:

            @pl.when(jnp.logical_and(row == source_row, col == last_col))
            def _():
                for copy in first_sends(slot):
                    copy.wait_send()

        for j, c in enumerate(other_cols):
            remote(g_mine, g_mine, send_line.at[j], recv_line, row, c).wait_send()


def share_g(rhs_last, row_count, col_count):
    size = rhs_last.shape[0]
    dma = pltpu.SemaphoreType.DMA
    peers = row_count - 1
    return pl.pallas_call(
        functools.partial(g_kernel, row_count, col_count),
        out_shape=jax.ShapeDtypeStruct((2, size, size), jnp.float32),
        in_specs=[pl.BlockSpec(memory_space=pl.ANY)],
        out_specs=pl.BlockSpec(memory_space=pltpu.VMEM),
        scratch_shapes=[
            dma((2, 2 * peers + 1)), dma((col_count // 2,)), dma((peers,)), dma((row_count,)),
            dma((2,)), dma, dma((row_count,)), dma((row_count,)), dma((2,)),
        ],
        compiler_params=pltpu.CompilerParams(
            collective_id=0, has_side_effects=True, vmem_limit_bytes=VMEM_LIMIT
        ),
        cost_estimate=pl.CostEstimate(flops=0, bytes_accessed=60_000_000, transcendentals=0),
    )(rhs_last)


def chain_of(row, source, backward, row_count):
    place = jnp.int32(0)
    after = jnp.int32(0)
    for s in range(row_count):
        forward = [s ^ (i ^ (i >> 1)) for i in range(row_count)]
        for b, order in enumerate((forward, forward[:1] + forward[:0:-1])):
            for i, r in enumerate(order):
                hit = jnp.logical_and(jnp.logical_and(source == s, backward == b), row == r)
                place = jnp.where(hit, i, place)
                after = jnp.where(hit, order[(i + 1) % row_count], after)
    return place, after


def run_chains(chains, row, col, row_count, on_arrival):
    for n in range(len(chains[0][3])):
        for place, after, start, landings, send, recv in chains:

            @pl.when(place == 0)
            def _():
                start(n, after)

    for n in range(len(chains[0][3])):
        for which, (place, after, start, landings, send, recv) in enumerate(chains):
            dst = landings[n]

            @pl.when(place > 0)
            def _():
                remote(dst, dst, send.at[n], recv.at[n], after, col).wait_recv()

                @pl.when(place < row_count - 1)
                def _():
                    remote(dst, dst, send.at[n], recv.at[n], after, col).start()

                on_arrival(which, n)

    for place, after, start, landings, send, recv in chains:

        @pl.when(place < row_count - 1)
        def _():
            for n, dst in enumerate(landings):
                remote(dst, dst, send.at[n], recv.at[n], after, col).wait_send()


def corner_kernel(
    row_count, last_ref, upper, lower, send, recv, sibling_send, sibling_recv, local_sem
):
    row = lax.axis_index("row")
    col = lax.axis_index("col")
    core = lax.rem(col, 2)
    sibling = col + 1 - 2 * core
    size = last_ref.shape[1]
    half = size // 2
    part = half // CORNER_PARTS
    greet([(r, col) for r in other_rows_of(row, row_count)] + [(row, sibling)])
    sources = (
        (row_count - 2, last_ref, upper),
        (row_count - 1, last_ref.at[:, :, pl.ds(size, size)], lower),
    )
    for slot, (source_row, src, out) in enumerate(sources):

        @pl.when(row == source_row)
        def _():
            pltpu.make_async_copy(src, out, local_sem.at[slot]).start()

    def rows_at(which_half, p):
        return pl.ds(pl.multiple_of(which_half * half + p * part, part), part)

    chains = []
    arriving = []
    for slot, (source_row, src, out) in enumerate(sources):
        for way in range(2):
            index = 2 * slot + way
            place, after = chain_of(row, source_row, way, row_count)

            def start(n, to, index=index, way=way, src=src, out=out):
                rows = rows_at(core, n)
                remote(
                    src.at[way, rows, :], out.at[way, rows, :],
                    send.at[index, n], recv.at[index, n], to, col,
                ).start()

            landings = [out.at[way, rows_at(core, n), :] for n in range(CORNER_PARTS)]
            arriving.append([out.at[way, rows_at(1 - core, n), :] for n in range(CORNER_PARTS)])
            chains.append((place, after, start, landings, send.at[index], recv.at[index]))

    def to_sibling(which, n):
        dst = chains[which][3][n]
        remote(dst, dst, sibling_send.at[which, n], sibling_recv.at[which, n], row, sibling).start()

    run_chains(chains, row, col, row_count, to_sibling)

    for which, chain in enumerate(chains):

        @pl.when(chain[0] > 0)
        def _():
            for n, ref in enumerate(arriving[which]):
                done = remote(
                    ref, ref, sibling_send.at[which, n], sibling_recv.at[which, n], row, sibling
                )
                done.wait_recv()
                done.wait_send()

    for slot, (source_row, src, out) in enumerate(sources):

        @pl.when(row == source_row)
        def _():
            pltpu.make_async_copy(src, out, local_sem.at[slot]).wait()


def share_corner(last_rows, row_count):
    _, size, width = last_rows.shape
    dma = pltpu.SemaphoreType.DMA
    return pl.pallas_call(
        functools.partial(corner_kernel, row_count),
        out_shape=(
            jax.ShapeDtypeStruct((2, size, width), jnp.bfloat16),
            jax.ShapeDtypeStruct((2, size, size), jnp.bfloat16),
        ),
        in_specs=[pl.BlockSpec(memory_space=pl.ANY)],
        out_specs=[pl.BlockSpec(memory_space=pltpu.VMEM)] * 2,
        scratch_shapes=[dma((4, CORNER_PARTS))] * 4 + [dma((2,))],
        compiler_params=pltpu.CompilerParams(
            collective_id=2, has_side_effects=True, vmem_limit_bytes=VMEM_LIMIT
        ),
        cost_estimate=pl.CostEstimate(flops=0, bytes_accessed=60_000_000, transcendentals=0),
    )(last_rows)


def mm(left, right):
    return lax.dot_general(left, right, (((1,), (0,)), ((), ())), preferred_element_type=jnp.float32)


def mm_t(left, right):
    return lax.dot_general(left, right, (((1,), (1,)), ((), ())), preferred_element_type=jnp.float32)


def split(value):
    high = value.astype(jnp.bfloat16)
    low = (value - high.astype(jnp.float32)).astype(jnp.bfloat16)
    return high, low


def upper_times(tri, parts):
    half = tri[0].shape[0] // 2
    top = bottom = None
    for i, t in enumerate(tri):
        for j, p in enumerate(parts):
            if i + j < 2:
                a = mm(t[:half], p)
                b = mm(t[half:, half:], p[half:])
                top = a if top is None else top + a
                bottom = b if bottom is None else bottom + b
    return jnp.concatenate([top, bottom], 0)


def times_upper_t(parts, tri):
    half = tri[0].shape[0] // 2
    left = right = None
    for i, t in enumerate(tri):
        for j, p in enumerate(parts):
            if i + j < 2:
                a = mm_t(p, t[:half])
                b = mm_t(p[:, half:], t[half:, half:])
                left = a if left is None else left + a
                right = b if right is None else right + b
    return jnp.concatenate([left, right], 1)


def solve_kernel(upper, lower, g, inverses, out, inv_high, inv_low):
    size = g.shape[1]
    for i in range(3):
        high, low = split(inverses[i])
        inv_high[i] = high
        inv_low[i] = low

    def precondition(i, residual):
        first = upper_times((inv_high[i], inv_low[i]), split(residual))
        return times_upper_t(split(first), (inv_high[2], inv_low[2]))

    def corner_update(residual):
        update = precondition(1, residual)
        return 0.25 * (update + update.T)

    out[0] = corner_update(-g[1])

    def corner_sweep(_, carry):
        first = upper_times((lower[0],), split(out[0]))
        term = times_upper_t(split(first), (lower[1],))
        out[0] = out[0] + corner_update(-g[1] - (term + term.T))
        return carry

    lax.fori_loop(1, SWEEPS, corner_sweep, 0)

    parts = split(out[0])
    over_a = split(sum(mm(upper[0, :, size:], p) for p in parts))
    over_e = split(sum(mm(upper[1, :, size:], p) for p in parts))
    g[0] = -g[0] - (times_upper_t(over_a, (lower[1],)) + times_upper_t(over_e, (lower[0],)))
    out[1] = 0.5 * precondition(0, g[0])

    def upper_sweep(_, carry):
        held = split(out[1])
        by_a = split(upper_times((upper[0, :, :size],), held))
        by_e = split(upper_times((upper[1, :, :size],), held))
        term = times_upper_t(by_a, (lower[1],)) + times_upper_t(by_e, (lower[0],))
        out[1] = out[1] + 0.5 * precondition(0, g[0] - term)
        return carry

    lax.fori_loop(1, SWEEPS, upper_sweep, 0)


def solve(upper, lower, g, inverses):
    size = g.shape[1]
    return pl.pallas_call(
        solve_kernel,
        out_shape=jax.ShapeDtypeStruct((2, size, size), jnp.float32),
        in_specs=[pl.BlockSpec(memory_space=pltpu.VMEM)] * 4,
        out_specs=pl.BlockSpec(memory_space=pltpu.VMEM),
        scratch_shapes=[
            pltpu.VMEM((3, size, size), jnp.bfloat16),
            pltpu.VMEM((3, size, size), jnp.bfloat16),
        ],
        compiler_params=pltpu.CompilerParams(vmem_limit_bytes=VMEM_LIMIT),
        cost_estimate=pl.CostEstimate(
            flops=100 * size ** 3, bytes_accessed=100_000_000, transcendentals=0
        ),
    )(upper, lower, g, inverses)


def column_kernel(row_count, col_count, rest_ref, last_ref, out, send, recv, local_sem):
    row = lax.axis_index("row")
    col = lax.axis_index("col")
    matrices, blocks, size, _ = out.shape
    part = size // COLUMN_PARTS
    group = col_count // row_count
    last_block = rest_ref.shape[1]
    greet([(r, col) for r in other_rows_of(row, row_count)])
    source = lax.rem(col, row_count)

    def from_block(b, use):
        block = col // row_count + b * group
        if (b + 1) * group > last_block:

            @pl.when(block == last_block)
            def _():
                use(last_ref)

            @pl.when(block < last_block)
            def _():
                use(rest_ref.at[:, jnp.minimum(block, last_block - 1)])

        else:
            use(rest_ref.at[:, block])

    pieces = [(b, p) for b in range(blocks) for p in range(COLUMN_PARTS)]
    chains = []
    for way in range(2):
        place, after = chain_of(row, source, way, row_count)

        def start(n, to, way=way):
            b, p = pieces[n]
            rows = pl.ds(p * part, part)
            from_block(
                b,
                lambda src: remote(
                    src.at[way, rows, :], out.at[way, b, rows, :],
                    send.at[way, n], recv.at[way, n], to, col,
                ).start(),
            )

        landings = [out.at[way, b, pl.ds(p * part, part), :] for b, p in pieces]
        chains.append((place, after, start, landings, send.at[way], recv.at[way]))

    def own(b, act):
        from_block(b, lambda src: act(pltpu.make_async_copy(src, out.at[:, b], local_sem.at[b])))

    @pl.when(row == source)
    def _():
        for b in range(blocks):
            own(b, lambda copy: copy.start())

    run_chains(chains, row, col, row_count, lambda which, n: None)

    @pl.when(row == source)
    def _():
        for b in range(blocks):
            own(b, lambda copy: copy.wait())


def share_columns(rest, last, col_blocks, row_count, col_count):
    matrices, _, size, width = rest.shape
    dma = pltpu.SemaphoreType.DMA
    return pl.pallas_call(
        functools.partial(column_kernel, row_count, col_count),
        out_shape=jax.ShapeDtypeStruct((matrices, col_blocks, size, width), rest.dtype),
        in_specs=[pl.BlockSpec(memory_space=pl.ANY)] * 2,
        out_specs=pl.BlockSpec(memory_space=pltpu.VMEM),
        scratch_shapes=[dma((2, col_blocks * COLUMN_PARTS))] * 2 + [dma((col_blocks,))],
        compiler_params=pltpu.CompilerParams(
            collective_id=1, has_side_effects=True, vmem_limit_bytes=VMEM_LIMIT
        ),
        cost_estimate=pl.CostEstimate(flops=0, bytes_accessed=60_000_000, transcendentals=0),
    )(rest, last)


def update_kernel(
    rest_steps, rest_ref, last_ref, cols_ref, x_ref, rhs_ref, out_ref, x_high, x_turned, z_cols
):
    step = pl.program_id(0)
    size = x_ref.shape[1]
    tile = rest_ref.shape[1]
    groups = rhs_ref.shape[0] // tile

    def times_known(left):
        from_right = left[:, size:]
        first = mm(from_right, x_turned[...])
        second = mm(left[:, :size], x_high[1]) + mm(from_right, x_high[0])
        return jnp.concatenate([first, second], 1).astype(jnp.bfloat16)

    @pl.when(step == 0)
    def _():
        x_high[...] = x_ref[...].astype(jnp.bfloat16)
        x_turned[...] = x_ref[1].T.astype(jnp.bfloat16)
        for b in range(z_cols.shape[0]):
            z_cols[b] = times_known(cols_ref[0, b])

    def work(rows_ref):
        z_rows = times_known(rows_ref[0])
        for b in range(z_cols.shape[0]):
            total = mm_t(z_rows, cols_ref[1, b]) + mm_t(rows_ref[1], z_cols[b])
            for q in range(size // LANES):
                where = pl.ds(b * (size // LANES) + q, tile, stride=groups)
                out_ref[where, :] = rhs_ref[where, :] + total[:, q * LANES:(q + 1) * LANES]

    @pl.when(step < rest_steps)
    def _():
        work(rest_ref)

    @pl.when(step >= rest_steps)
    def _():
        work(last_ref)


def update(rest, last, cols, x, rhs):
    size = x.shape[1]
    width = rest.shape[-1]
    blocks = cols.shape[1]
    rest_rows = rest.reshape(2, -1, width)
    tile = size // 2
    groups = blocks * size // LANES
    rest_steps = rest_rows.shape[1] // tile
    steps = rest_steps + last.shape[1] // tile
    flat = rhs.reshape(-1, LANES)
    out = pl.pallas_call(
        functools.partial(update_kernel, rest_steps),
        grid=(steps,),
        out_shape=jax.ShapeDtypeStruct(flat.shape, flat.dtype),
        in_specs=[
            pl.BlockSpec((2, tile, width), lambda i: (0, jnp.minimum(i, rest_steps - 1), 0)),
            pl.BlockSpec((2, tile, width), lambda i: (0, jnp.maximum(i - rest_steps, 0), 0)),
            pl.BlockSpec(cols.shape, lambda i: (0, 0, 0, 0)),
            pl.BlockSpec(x.shape, lambda i: (0, 0, 0)),
            pl.BlockSpec((tile * groups, LANES), lambda i: (i, 0)),
        ],
        out_specs=pl.BlockSpec((tile * groups, LANES), lambda i: (i, 0)),
        scratch_shapes=[
            pltpu.VMEM((2, size, size), jnp.bfloat16),
            pltpu.VMEM((size, size), jnp.bfloat16),
            pltpu.VMEM((blocks, size, width), jnp.bfloat16),
        ],
        compiler_params=pltpu.CompilerParams(vmem_limit_bytes=VMEM_LIMIT),
    )(rest_rows, last, cols, x, flat)
    return out.reshape(rhs.shape)


def on_device(rhs, panels, inverses):
    row_index = lax.axis_index("row")
    col_index = lax.axis_index("col")
    row_count = lax.axis_size("row")
    col_count = lax.axis_size("col")
    blocks_here = panels.shape[1]
    col_blocks = rhs.shape[3]
    size = rhs.shape[-1]
    last = lax.all_gather(panels[:, blocks_here - 1, 0], "col", axis=1, tiled=True)
    rhs_last = rhs[blocks_here - 1, 0, :, col_blocks - 1, 0, :]
    g = share_g(rhs_last, row_count, col_count)
    rest_here, last, g = lax.optimization_barrier((panels[:, : blocks_here - 1, 0], last, g))
    rest = lax.all_gather(rest_here, "col", axis=2, tiled=True)
    upper, lower = share_corner(last, row_count)
    x = solve(upper, lower, g, inverses)
    cols = share_columns(rest, last, col_blocks, row_count, col_count)
    new_rhs = update(rest, last, cols, x, rhs)
    rows_part = size // row_count
    cols_part = size // col_count
    solved = lax.dynamic_slice(
        x, (0, row_index * rows_part, col_index * cols_part), (2, rows_part, cols_part)
    )
    return (new_rhs, solved)


def solution(mesh):
    in_specs = (P(None, "row", None, None, "col", None), P(None, None, "row", "col", None), P())
    out_specs = (P(None, "row", None, None, "col", None), P(None, "row", "col"))
    return jax.shard_map(
        on_device, mesh=mesh, in_specs=in_specs, out_specs=out_specs, check_vma=False
    )
```

```python
import functools

import jax
import jax.numpy as jnp
from jax import lax
from jax.experimental import pallas as pl
from jax.experimental.pallas import tpu as pltpu
from jax.sharding import PartitionSpec as P

SWEEPS = 3
LANES = 128
MESH = pl.DeviceIdType.MESH
CORNER_PARTS = 4
COLUMN_PARTS = 4
VMEM_LIMIT = 50 * 1024 * 1024


def remote(src, dst, send_sem, recv_sem, row, col):
    return pltpu.make_async_remote_copy(
        src_ref=src, dst_ref=dst, send_sem=send_sem, recv_sem=recv_sem,
        device_id=(row, col), device_id_type=MESH,
    )


def greet(partners):
    barrier = pltpu.get_barrier_semaphore()
    for row, col in partners:
        pl.semaphore_signal(barrier, inc=1, device_id=(row, col), device_id_type=MESH)
    pl.semaphore_wait(barrier, len(partners))


def other_rows_of(row, row_count):
    return [lax.rem(row + j, row_count) for j in range(1, row_count)]


def g_kernel(
    row_count, col_count, g_ref, g_out,
    send_first, send_line, send_rows, send_sibling,
    recv_first, recv_line, recv_rows, recv_sibling, local_sem,
):
    row = lax.axis_index("row")
    col = lax.axis_index("col")
    core = lax.rem(col, 2)
    sibling = col + 1 - 2 * core
    part = g_ref.shape[0] // (2 * row_count)
    last_col = col_count - 1
    other_rows = other_rows_of(row, row_count)
    other_cols = [lax.rem(col + 2 * j, col_count) for j in range(1, col_count // 2)]
    on_last_chip = col >= last_col - 1
    greet(
        [(r, col) for r in other_rows]
        + [(r, sibling) for r in other_rows]
        + [(row, c) for c in other_cols]
        + [(row, sibling)]
    )

    def rows_of(r, k):
        return pl.ds(pl.multiple_of((2 * r + k) * part, part), part)

    mine = rows_of(row, core)
    g_mine = g_out.at[:, mine, :]
    sources = ((row_count - 2, 0), (row_count - 1, 1))

    def first_sends(slot):
        for j, (r, k) in enumerate(
            [(r, k) for r in other_rows for k in range(2)] + [(row, 0)]
        ):
            theirs = rows_of(r, k)
            yield remote(
                g_ref.at[theirs, :], g_out.at[slot, theirs, :],
                send_first.at[slot, j], recv_first.at[slot], r, last_col - 1 + k,
            )

    @pl.when(on_last_chip)
    def _():
        for source_row, slot in sources:

            @pl.when(jnp.logical_and(row == source_row, col == last_col))
            def _():
                pltpu.make_async_copy(
                    g_ref.at[mine, :], g_out.at[slot, mine, :], local_sem.at[slot]
                ).start()
                for copy in first_sends(slot):
                    copy.start()

        for source_row, slot in sources:
            piece = g_out.at[slot, mine, :]
            holder = jnp.logical_and(row == source_row, col == last_col)

            @pl.when(holder)
            def _():
                pltpu.make_async_copy(g_ref.at[mine, :], piece, local_sem.at[slot]).wait()

            @pl.when(jnp.logical_not(holder))
            def _():
                remote(piece, piece, send_first.at[slot, 0], recv_first.at[slot], row, col).wait_recv()

        for j, c in enumerate(other_cols):
            remote(g_mine, g_mine, send_line.at[j], recv_line, row, c).start()

    @pl.when(jnp.logical_not(on_last_chip))
    def _():
        remote(g_mine, g_mine, send_line.at[0], recv_line, row, col).wait_recv()

    for j, r in enumerate(other_rows):
        remote(g_mine, g_mine, send_rows.at[j], recv_rows.at[row], r, col).start()
    remote(g_mine, g_mine, send_sibling.at[row], recv_sibling.at[row], row, sibling).start()
    for r in other_rows:
        piece = g_out.at[:, rows_of(r, core), :]
        remote(piece, piece, send_rows.at[0], recv_rows.at[r], row, col).wait_recv()
        remote(piece, piece, send_sibling.at[r], recv_sibling.at[r], row, sibling).start()
    for r in [row] + other_rows:
        piece = g_out.at[:, rows_of(r, 1 - core), :]
        remote(piece, piece, send_sibling.at[r], recv_sibling.at[r], row, sibling).wait_recv()
        remote(piece, piece, send_sibling.at[r], recv_sibling.at[r], row, sibling).wait_send()
    for j, r in enumerate(other_rows):
        remote(g_mine, g_mine, send_rows.at[j], recv_rows.at[row], r, col).wait_send()

    @pl.when(on_last_chip)
    def _():
        for source_row, slot in sources:

            @pl.when(jnp.logical_and(row == source_row, col == last_col))
            def _():
                for copy in first_sends(slot):
                    copy.wait_send()

        for j, c in enumerate(other_cols):
            remote(g_mine, g_mine, send_line.at[j], recv_line, row, c).wait_send()


def share_g(rhs_last, row_count, col_count):
    size = rhs_last.shape[0]
    dma = pltpu.SemaphoreType.DMA
    peers = row_count - 1
    return pl.pallas_call(
        functools.partial(g_kernel, row_count, col_count),
        out_shape=jax.ShapeDtypeStruct((2, size, size), jnp.float32),
        in_specs=[pl.BlockSpec(memory_space=pl.ANY)],
        out_specs=pl.BlockSpec(memory_space=pltpu.VMEM),
        scratch_shapes=[
            dma((2, 2 * peers + 1)), dma((col_count // 2,)), dma((peers,)), dma((row_count,)),
            dma((2,)), dma, dma((row_count,)), dma((row_count,)), dma((2,)),
        ],
        compiler_params=pltpu.CompilerParams(
            collective_id=0, has_side_effects=True, vmem_limit_bytes=VMEM_LIMIT
        ),
        cost_estimate=pl.CostEstimate(flops=0, bytes_accessed=60_000_000, transcendentals=0),
    )(rhs_last)


def chain_of(row, source, backward, row_count):
    place = jnp.int32(0)
    after = jnp.int32(0)
    for s in range(row_count):
        forward = [s ^ (i ^ (i >> 1)) for i in range(row_count)]
        for b, order in enumerate((forward, forward[:1] + forward[:0:-1])):
            for i, r in enumerate(order):
                hit = jnp.logical_and(jnp.logical_and(source == s, backward == b), row == r)
                place = jnp.where(hit, i, place)
                after = jnp.where(hit, order[(i + 1) % row_count], after)
    return place, after


def run_chains(chains, row, col, row_count, on_arrival):
    for n in range(len(chains[0][3])):
        for place, after, start, landings, send, recv in chains:

            @pl.when(place == 0)
            def _():
                start(n, after)

    count = len(chains[0][3])
    for step in range(1, count + row_count - 1):
        for which, (place, after, start, landings, send, recv) in enumerate(chains):
            for at in range(max(1, step - count + 1), min(step, row_count - 1) + 1):
                n = step - at
                dst = landings[n]

                @pl.when(place == at)
                def _():
                    remote(dst, dst, send.at[n], recv.at[n], after, col).wait_recv()
                    if at < row_count - 1:
                        remote(dst, dst, send.at[n], recv.at[n], after, col).start()
                    on_arrival(which, n)

    for place, after, start, landings, send, recv in chains:

        @pl.when(place < row_count - 1)
        def _():
            for n, dst in enumerate(landings):
                remote(dst, dst, send.at[n], recv.at[n], after, col).wait_send()


def corner_kernel(
    row_count, last_ref, upper, lower, send, recv, sibling_send, sibling_recv, local_sem
):
    row = lax.axis_index("row")
    col = lax.axis_index("col")
    core = lax.rem(col, 2)
    sibling = col + 1 - 2 * core
    size = last_ref.shape[1]
    half = size // 2
    part = half // CORNER_PARTS
    greet([(r, col) for r in other_rows_of(row, row_count)] + [(row, sibling)])
    sources = (
        (row_count - 2, last_ref, upper),
        (row_count - 1, last_ref.at[:, :, pl.ds(size, size)], lower),
    )
    for slot, (source_row, src, out) in enumerate(sources):

        @pl.when(row == source_row)
        def _():
            pltpu.make_async_copy(src, out, local_sem.at[slot]).start()

    def rows_at(which_half, p):
        return pl.ds(pl.multiple_of(which_half * half + p * part, part), part)

    chains = []
    arriving = []
    for slot, (source_row, src, out) in enumerate(sources):
        for way in range(2):
            index = 2 * slot + way
            place, after = chain_of(row, source_row, way, row_count)

            def start(n, to, index=index, way=way, src=src, out=out):
                rows = rows_at(core, n)
                remote(
                    src.at[way, rows, :], out.at[way, rows, :],
                    send.at[index, n], recv.at[index, n], to, col,
                ).start()

            landings = [out.at[way, rows_at(core, n), :] for n in range(CORNER_PARTS)]
            arriving.append([out.at[way, rows_at(1 - core, n), :] for n in range(CORNER_PARTS)])
            chains.append((place, after, start, landings, send.at[index], recv.at[index]))

    def to_sibling(which, n):
        dst = chains[which][3][n]
        remote(dst, dst, sibling_send.at[which, n], sibling_recv.at[which, n], row, sibling).start()

    run_chains(chains, row, col, row_count, to_sibling)

    for which, chain in enumerate(chains):

        @pl.when(chain[0] > 0)
        def _():
            for n, ref in enumerate(arriving[which]):
                done = remote(
                    ref, ref, sibling_send.at[which, n], sibling_recv.at[which, n], row, sibling
                )
                done.wait_recv()
                done.wait_send()

    for slot, (source_row, src, out) in enumerate(sources):

        @pl.when(row == source_row)
        def _():
            pltpu.make_async_copy(src, out, local_sem.at[slot]).wait()


def share_corner(last_rows, row_count):
    _, size, width = last_rows.shape
    dma = pltpu.SemaphoreType.DMA
    return pl.pallas_call(
        functools.partial(corner_kernel, row_count),
        out_shape=(
            jax.ShapeDtypeStruct((2, size, width), jnp.bfloat16),
            jax.ShapeDtypeStruct((2, size, size), jnp.bfloat16),
        ),
        in_specs=[pl.BlockSpec(memory_space=pl.ANY)],
        out_specs=[pl.BlockSpec(memory_space=pltpu.VMEM)] * 2,
        scratch_shapes=[dma((4, CORNER_PARTS))] * 4 + [dma((2,))],
        compiler_params=pltpu.CompilerParams(
            collective_id=2, has_side_effects=True, vmem_limit_bytes=VMEM_LIMIT
        ),
        cost_estimate=pl.CostEstimate(flops=0, bytes_accessed=60_000_000, transcendentals=0),
    )(last_rows)


def mm(left, right):
    return lax.dot_general(left, right, (((1,), (0,)), ((), ())), preferred_element_type=jnp.float32)


def mm_t(left, right):
    return lax.dot_general(left, right, (((1,), (1,)), ((), ())), preferred_element_type=jnp.float32)


def split(value):
    high = value.astype(jnp.bfloat16)
    low = (value - high.astype(jnp.float32)).astype(jnp.bfloat16)
    return high, low


def upper_times(tri, parts):
    half = tri[0].shape[0] // 2
    top = bottom = None
    for i, t in enumerate(tri):
        for j, p in enumerate(parts):
            if i + j < 2:
                a = mm(t[:half], p)
                b = mm(t[half:, half:], p[half:])
                top = a if top is None else top + a
                bottom = b if bottom is None else bottom + b
    return jnp.concatenate([top, bottom], 0)


def times_upper_t(parts, tri):
    half = tri[0].shape[0] // 2
    left = right = None
    for i, t in enumerate(tri):
        for j, p in enumerate(parts):
            if i + j < 2:
                a = mm_t(p, t[:half])
                b = mm_t(p[:, half:], t[half:, half:])
                left = a if left is None else left + a
                right = b if right is None else right + b
    return jnp.concatenate([left, right], 1)


def solve_kernel(upper, lower, g, inverses, out, inv_high, inv_low):
    size = g.shape[1]
    for i in range(3):
        high, low = split(inverses[i])
        inv_high[i] = high
        inv_low[i] = low

    def precondition(i, residual):
        first = upper_times((inv_high[i], inv_low[i]), split(residual))
        return times_upper_t(split(first), (inv_high[2], inv_low[2]))

    def corner_update(residual):
        update = precondition(1, residual)
        return 0.25 * (update + update.T)

    out[0] = corner_update(-g[1])

    def corner_sweep(_, carry):
        first = upper_times((lower[0],), split(out[0]))
        term = times_upper_t(split(first), (lower[1],))
        out[0] = out[0] + corner_update(-g[1] - (term + term.T))
        return carry

    lax.fori_loop(1, SWEEPS, corner_sweep, 0)

    parts = split(out[0])
    over_a = split(sum(mm(upper[0, :, size:], p) for p in parts))
    over_e = split(sum(mm(upper[1, :, size:], p) for p in parts))
    g[0] = -g[0] - (times_upper_t(over_a, (lower[1],)) + times_upper_t(over_e, (lower[0],)))
    out[1] = 0.5 * precondition(0, g[0])

    def upper_sweep(_, carry):
        held = split(out[1])
        by_a = split(upper_times((upper[0, :, :size],), held))
        by_e = split(upper_times((upper[1, :, :size],), held))
        term = times_upper_t(by_a, (lower[1],)) + times_upper_t(by_e, (lower[0],))
        out[1] = out[1] + 0.5 * precondition(0, g[0] - term)
        return carry

    lax.fori_loop(1, SWEEPS, upper_sweep, 0)


def solve(upper, lower, g, inverses):
    size = g.shape[1]
    return pl.pallas_call(
        solve_kernel,
        out_shape=jax.ShapeDtypeStruct((2, size, size), jnp.float32),
        in_specs=[pl.BlockSpec(memory_space=pltpu.VMEM)] * 4,
        out_specs=pl.BlockSpec(memory_space=pltpu.VMEM),
        scratch_shapes=[
            pltpu.VMEM((3, size, size), jnp.bfloat16),
            pltpu.VMEM((3, size, size), jnp.bfloat16),
        ],
        compiler_params=pltpu.CompilerParams(vmem_limit_bytes=VMEM_LIMIT),
        cost_estimate=pl.CostEstimate(
            flops=100 * size ** 3, bytes_accessed=100_000_000, transcendentals=0
        ),
    )(upper, lower, g, inverses)


def column_kernel(row_count, col_count, rest_ref, last_ref, out, send, recv, local_sem):
    row = lax.axis_index("row")
    col = lax.axis_index("col")
    matrices, blocks, size, _ = out.shape
    part = size // COLUMN_PARTS
    group = col_count // row_count
    last_block = rest_ref.shape[1]
    greet([(r, col) for r in other_rows_of(row, row_count)])
    source = lax.rem(col, row_count)

    def from_block(b, use):
        block = col // row_count + b * group
        if (b + 1) * group > last_block:

            @pl.when(block == last_block)
            def _():
                use(last_ref)

            @pl.when(block < last_block)
            def _():
                use(rest_ref.at[:, jnp.minimum(block, last_block - 1)])

        else:
            use(rest_ref.at[:, block])

    pieces = [(b, p) for b in range(blocks) for p in range(COLUMN_PARTS)]
    chains = []
    for way in range(2):
        place, after = chain_of(row, source, way, row_count)

        def start(n, to, way=way):
            b, p = pieces[n]
            rows = pl.ds(p * part, part)
            from_block(
                b,
                lambda src: remote(
                    src.at[way, rows, :], out.at[way, b, rows, :],
                    send.at[way, n], recv.at[way, n], to, col,
                ).start(),
            )

        landings = [out.at[way, b, pl.ds(p * part, part), :] for b, p in pieces]
        chains.append((place, after, start, landings, send.at[way], recv.at[way]))

    def own(b, act):
        from_block(b, lambda src: act(pltpu.make_async_copy(src, out.at[:, b], local_sem.at[b])))

    @pl.when(row == source)
    def _():
        for b in range(blocks):
            own(b, lambda copy: copy.start())

    run_chains(chains, row, col, row_count, lambda which, n: None)

    @pl.when(row == source)
    def _():
        for b in range(blocks):
            own(b, lambda copy: copy.wait())


def share_columns(rest, last, col_blocks, row_count, col_count):
    matrices, _, size, width = rest.shape
    dma = pltpu.SemaphoreType.DMA
    return pl.pallas_call(
        functools.partial(column_kernel, row_count, col_count),
        out_shape=jax.ShapeDtypeStruct((matrices, col_blocks, size, width), rest.dtype),
        in_specs=[pl.BlockSpec(memory_space=pl.ANY)] * 2,
        out_specs=pl.BlockSpec(memory_space=pltpu.VMEM),
        scratch_shapes=[dma((2, col_blocks * COLUMN_PARTS))] * 2 + [dma((col_blocks,))],
        compiler_params=pltpu.CompilerParams(
            collective_id=1, has_side_effects=True, vmem_limit_bytes=VMEM_LIMIT
        ),
        cost_estimate=pl.CostEstimate(flops=0, bytes_accessed=60_000_000, transcendentals=0),
    )(rest, last)


def update_kernel(
    rest_steps, rest_ref, last_ref, cols_ref, x_ref, rhs_ref, out_ref, x_high, x_turned, z_cols
):
    step = pl.program_id(0)
    size = x_ref.shape[1]
    tile = rest_ref.shape[1]
    groups = rhs_ref.shape[0] // tile

    def times_known(left):
        from_right = left[:, size:]
        first = mm(from_right, x_turned[...])
        second = mm(left[:, :size], x_high[1]) + mm(from_right, x_high[0])
        return jnp.concatenate([first, second], 1).astype(jnp.bfloat16)

    @pl.when(step == 0)
    def _():
        x_high[...] = x_ref[...].astype(jnp.bfloat16)
        x_turned[...] = x_ref[1].T.astype(jnp.bfloat16)
        for b in range(z_cols.shape[0]):
            z_cols[b] = times_known(cols_ref[0, b])

    def work(rows_ref):
        z_rows = times_known(rows_ref[0])
        for b in range(z_cols.shape[0]):
            total = mm_t(z_rows, cols_ref[1, b]) + mm_t(rows_ref[1], z_cols[b])
            for q in range(size // LANES):
                where = pl.ds(b * (size // LANES) + q, tile, stride=groups)
                out_ref[where, :] = rhs_ref[where, :] + total[:, q * LANES:(q + 1) * LANES]

    @pl.when(step < rest_steps)
    def _():
        work(rest_ref)

    @pl.when(step >= rest_steps)
    def _():
        work(last_ref)


def update(rest, last, cols, x, rhs):
    size = x.shape[1]
    width = rest.shape[-1]
    blocks = cols.shape[1]
    rest_rows = rest.reshape(2, -1, width)
    tile = size // 2
    groups = blocks * size // LANES
    rest_steps = rest_rows.shape[1] // tile
    steps = rest_steps + last.shape[1] // tile
    flat = rhs.reshape(-1, LANES)
    out = pl.pallas_call(
        functools.partial(update_kernel, rest_steps),
        grid=(steps,),
        out_shape=jax.ShapeDtypeStruct(flat.shape, flat.dtype),
        in_specs=[
            pl.BlockSpec((2, tile, width), lambda i: (0, jnp.minimum(i, rest_steps - 1), 0)),
            pl.BlockSpec((2, tile, width), lambda i: (0, jnp.maximum(i - rest_steps, 0), 0)),
            pl.BlockSpec(cols.shape, lambda i: (0, 0, 0, 0)),
            pl.BlockSpec(x.shape, lambda i: (0, 0, 0)),
            pl.BlockSpec((tile * groups, LANES), lambda i: (i, 0)),
        ],
        out_specs=pl.BlockSpec((tile * groups, LANES), lambda i: (i, 0)),
        scratch_shapes=[
            pltpu.VMEM((2, size, size), jnp.bfloat16),
            pltpu.VMEM((size, size), jnp.bfloat16),
            pltpu.VMEM((blocks, size, width), jnp.bfloat16),
        ],
        compiler_params=pltpu.CompilerParams(vmem_limit_bytes=VMEM_LIMIT),
    )(rest_rows, last, cols, x, flat)
    return out.reshape(rhs.shape)


def on_device(rhs, panels, inverses):
    row_index = lax.axis_index("row")
    col_index = lax.axis_index("col")
    row_count = lax.axis_size("row")
    col_count = lax.axis_size("col")
    blocks_here = panels.shape[1]
    col_blocks = rhs.shape[3]
    size = rhs.shape[-1]
    last = lax.all_gather(panels[:, blocks_here - 1, 0], "col", axis=1, tiled=True)
    rhs_last = rhs[blocks_here - 1, 0, :, col_blocks - 1, 0, :]
    g = share_g(rhs_last, row_count, col_count)
    rest_here, last, g = lax.optimization_barrier((panels[:, : blocks_here - 1, 0], last, g))
    rest = lax.all_gather(rest_here, "col", axis=2, tiled=True)
    upper, lower = share_corner(last, row_count)
    x = solve(upper, lower, g, inverses)
    cols = share_columns(rest, last, col_blocks, row_count, col_count)
    new_rhs = update(rest, last, cols, x, rhs)
    rows_part = size // row_count
    cols_part = size // col_count
    solved = lax.dynamic_slice(
        x, (0, row_index * rows_part, col_index * cols_part), (2, rows_part, cols_part)
    )
    return (new_rhs, solved)


def solution(mesh):
    in_specs = (P(None, "row", None, None, "col", None), P(None, None, "row", "col", None), P())
    out_specs = (P(None, "row", None, None, "col", None), P(None, "row", "col"))
    return jax.shard_map(
        on_device, mesh=mesh, in_specs=in_specs, out_specs=out_specs, check_vma=False
    )
```
